256 devices in a mesh: section: 16 (over x, y_hi, core), seq: 16 (over z, y_lo).
Axes of the slice: x: 4, y: 4 (y_hi: 2, y_lo: 2; y = y_hi * 2 + y_lo), z: 8, core: 2. Of those that a mesh axis runs over, the one named last changes fastest.
Arguments:
- grad_out: bfloat16 [16, 2048, 2048], P('section', 'seq'), may hold values from -6 to 6
- block_input: bfloat16 [16, 2048, 2048], P('section', 'seq'), may hold values from -5 to 5
- skip_saved: bfloat16 [16, 2048, 2048], P('section', 'seq'), may hold values from -2 to 2
- saved_qkv: bfloat16 [16, 3, 2048, 2048], P('section', None, None, 'seq'), may hold values from -16 to 16
- out_weight: bfloat16 [16, 2048, 2048], P('section', 'seq'), may hold values from -0.125 to 0.125
- qkv_weight: bfloat16 [16, 3, 2048, 2048], P('section', None, 'seq'), may hold values from -0.125 to 0.125
- gate: float32 [16, 2048], P('section'), may hold values from 0.5 to 1.5
- norm_scale: float32 [16, 2048], P('section'), may hold values from -0.5 to 0.5
- skip_gain: float32 [16, 2048], P('section'), may hold values from 0.3 to 1.5
Outputs:
- next_grad: bfloat16 [16, 2048, 2048], P('section', 'seq')
- down_grad: bfloat16 [16, 2048, 2048], P('section', 'seq')
- gain_grad: float32 [16, 2048], P('section')
The draws below stay inside these ranges and needn't reach their ends.
All inputs are finite; a program needn't handle non-finite values.
Results may differ from the reference program's by a relative error of at most 0.015.
Values may be sent and summed in bfloat16 or wider, within the bound.
A program may use at most 128 MiB of HBM per device.

```python
import math
import jax
import jax.numpy as jnp
from jax import lax

D = 2048
HEADS = 16
HEAD_DIM = 128
TOKENS = 2048
SECTIONS = 16
N_SEQ = 16


def draw_saved_qkv(key, part):
    width = HEADS * HEAD_DIM
    key_base = jax.random.fold_in(key, 0)
    values = jnp.clip(jax.random.normal(key_base, (SECTIONS, 3, TOKENS, width), jnp.float32), -4.0, 4.0)
    return values.astype(jnp.bfloat16)


def draw_block_input(key, part):
    key_base, key_rows, key_cols = jax.random.split(key, 3)
    row_scale = jnp.exp(jax.random.uniform(key_rows, (SECTIONS, TOKENS, 1), jnp.float32, math.log(0.01), math.log(0.1)))
    col_scale = jnp.exp(jax.random.uniform(key_cols, (SECTIONS, 1, D), jnp.float32, 0.0, math.log(10.0)))
    base = jnp.clip(jax.random.normal(key_base, (SECTIONS, TOKENS, D), jnp.float32), -4.0, 4.0)
    return (base * row_scale * col_scale).astype(jnp.bfloat16)


def draw_skip_saved(key, part):
    position = jnp.arange(TOKENS).astype(jnp.float32)[None, :, None]
    rising = (1.0 + 2.0 * position / (TOKENS - 1)) * TOKENS ** (-0.5)
    base = jnp.clip(jax.random.normal(key, (SECTIONS, TOKENS, D), jnp.float32), -4.0, 4.0)
    return jnp.clip(base * rising, -2.0, 2.0).astype(jnp.bfloat16)


def steps_of(rng, dims, cuts, least, largest):
    def one(dim, parts):
        steps = jax.random.uniform(jax.random.fold_in(jax.random.fold_in(rng, 6), dim), (parts,), jnp.float32, least / len(cuts), largest / len(cuts))
        return jnp.repeat(jnp.exp(steps), dims[dim] // parts).reshape((-1,) + (1,) * (len(dims) - dim - 1))

    loudness = one(*cuts[0])
    for cut in cuts[1:]:
        loudness = loudness * one(*cut)
    return loudness


def normal_values(rng, extent, spread, bound, shards=(), dtype=jnp.bfloat16):
    drawn = jax.random.normal(rng, extent, jnp.float32) * spread
    if len(shards) > 0:
        drawn = steps_of(rng, extent, shards, -0.22, 0.18) * drawn
    return jnp.clip(drawn, min=-bound, max=bound).astype(dtype)


def setup_inputs(seed: int = 0) -> dict:
    streams_of = jax.random.split(jax.random.key(seed), 10)
    return {
        "grad_out": normal_values(streams_of[0], (SECTIONS, TOKENS, D), 1.0, 6.0, ((0, 16), (1, 16))),
        "block_input": draw_block_input(jax.random.fold_in(streams_of[9], 71), 0),
        "skip_saved": draw_skip_saved(jax.random.fold_in(streams_of[9], 71), 0),
        "saved_qkv": draw_saved_qkv(jax.random.fold_in(streams_of[9], 71), 0),
        "out_weight": normal_values(streams_of[4], (SECTIONS, HEADS * HEAD_DIM, D), (HEADS * HEAD_DIM) ** -0.5, 0.125, ((0, 16), (1, 16))),
        "qkv_weight": normal_values(streams_of[5], (SECTIONS, 3, HEADS * HEAD_DIM, D), D ** -0.5, 0.125, ((0, 16), (2, 16))),
        "gate": jnp.clip(0.5 + 1.0 * jax.random.uniform(streams_of[6], (SECTIONS, D), jnp.float32) ** steps_of(streams_of[6], (SECTIONS, D), ((0, 16),), -0.2, 0.2), 0.5, 1.5),
        "norm_scale": jnp.clip(jax.random.uniform(streams_of[7], (SECTIONS, D), jnp.float32, -0.5, 0.5) * steps_of(streams_of[7], (SECTIONS, D), ((0, 16),), -0.4, 0.0), -0.5, 0.5),
        "skip_gain": jnp.clip(0.3 + 1.2 * jax.random.uniform(streams_of[8], (SECTIONS, D), jnp.float32) ** steps_of(streams_of[8], (SECTIONS, D), ((0, 16),), -0.2, 0.2), 0.3, 1.5),
    }


def head_backward(inputs):
    query, keys, values, grad_head = inputs
    factor = HEAD_DIM ** (-0.5)
    scores = jnp.dot(query, keys.T, preferred_element_type=jnp.float32) * factor
    scores = scores - lax.optimization_barrier(jnp.max(scores, axis=-1, keepdims=True))
    weights = jnp.exp(scores)
    probs = weights / lax.optimization_barrier(jnp.sum(weights, axis=-1, keepdims=True))
    dprobs = jnp.dot(grad_head, values.T, preferred_element_type=jnp.float32)
    delta = lax.optimization_barrier(jnp.sum(probs * dprobs, axis=-1, keepdims=True))
    dscores = probs * (dprobs - delta)
    probs_low = probs.astype(jnp.bfloat16)
    dscores_low = dscores.astype(jnp.bfloat16)
    grad_query = (jnp.dot(dscores_low, keys, preferred_element_type=jnp.float32) * factor).astype(jnp.bfloat16)
    grad_keys = (jnp.dot(dscores_low.T, query, preferred_element_type=jnp.float32) * factor).astype(jnp.bfloat16)
    grad_values = jnp.dot(probs_low.T, grad_head, preferred_element_type=jnp.float32).astype(jnp.bfloat16)
    return (grad_query, grad_keys, grad_values)

def add_feature(total, paired_values):
    partial_term = jnp.dot(paired_values[0], paired_values[1].T, preferred_element_type=jnp.float32)
    rounded = lax.optimization_barrier(partial_term.astype(jnp.bfloat16))
    return (total + rounded.astype(jnp.float32), None)

def add_heads(total, paired_values):
    partial_term = jnp.einsum('wqg,wgj->qj', paired_values[0].astype(jnp.float32), paired_values[1].astype(jnp.float32))
    rounded = lax.optimization_barrier(partial_term.astype(jnp.bfloat16))
    return (total + rounded.astype(jnp.float32), None)

def section_backward(inputs):
    incoming_gradient, block_in, skip_in, qkv_in, weight_out, weight_qkv, gate_row, scale_row, gain_row, last_flag = inputs
    width = HEADS * HEAD_DIM
    feat_group = D // N_SEQ
    head_group = HEADS // N_SEQ
    gated = (incoming_gradient.astype(jnp.float32) * gate_row).astype(jnp.bfloat16)
    gated_groups = jnp.moveaxis(gated.reshape(TOKENS, N_SEQ, feat_group), 1, 0)
    weight_groups = jnp.moveaxis(weight_out.reshape(width, N_SEQ, feat_group), 1, 0)
    summed, _ = lax.scan(add_feature, jnp.zeros((TOKENS, width), jnp.float32), (gated_groups, weight_groups))
    attn_grad = summed.astype(jnp.bfloat16)

    def by_heads(matrix):
        return jnp.moveaxis(matrix.reshape(TOKENS, HEADS, HEAD_DIM), 1, 0)
    grad_query, grad_keys, grad_values = lax.map(head_backward, (by_heads(qkv_in[0]), by_heads(qkv_in[1]), by_heads(qkv_in[2]), by_heads(attn_grad)))
    stacked = jnp.stack([grad_query, grad_keys, grad_values], 0)
    stacked = stacked.reshape(3, N_SEQ, head_group, TOKENS, HEAD_DIM)
    stacked = jnp.transpose(stacked, (1, 0, 3, 2, 4)).reshape(N_SEQ, 3, TOKENS, head_group * HEAD_DIM)
    weight_parts = jnp.moveaxis(weight_qkv.reshape(3, N_SEQ, head_group * HEAD_DIM, D), 1, 0)
    normed_grad, _ = lax.scan(add_heads, jnp.zeros((TOKENS, D), jnp.float32), (stacked, weight_parts))
    xval = block_in.astype(jnp.float32)
    mean_x = lax.optimization_barrier(jnp.mean(xval, axis=-1, keepdims=True))
    centered_input = xval - mean_x
    var_x = lax.optimization_barrier(jnp.mean(centered_input * centered_input, axis=-1, keepdims=True))
    inverse_deviation = 1.0 / jnp.sqrt(var_x + 1e-06)
    normalized_input = centered_input * inverse_deviation
    scaled_gradient = normed_grad * (1.0 + scale_row)
    input_gradient = incoming_gradient.astype(jnp.float32) + inverse_deviation * (scaled_gradient - lax.optimization_barrier(jnp.mean(scaled_gradient, axis=-1, keepdims=True)) - normalized_input * lax.optimization_barrier(jnp.mean(scaled_gradient * normalized_input, axis=-1, keepdims=True)))
    hand_grad = input_gradient.astype(jnp.bfloat16)
    mirror_grad = ((gain_row + last_flag) * input_gradient).astype(jnp.bfloat16)
    gain_grad = lax.optimization_barrier(jnp.sum(input_gradient * skip_in.astype(jnp.float32), axis=0))
    return (hand_grad, mirror_grad, gain_grad)

def reference(grad_out, block_input, skip_saved, saved_qkv, out_weight, qkv_weight, gate, norm_scale, skip_gain):
    last_flags = (jnp.arange(SECTIONS) == SECTIONS - 1).astype(jnp.float32)[:, None]
    hand_grad, down_grad, gain_grad = lax.map(section_backward, (grad_out, block_input, skip_saved, saved_qkv, out_weight, qkv_weight, gate, norm_scale, skip_gain, last_flags))
    next_grad = jnp.concatenate([jnp.zeros((1, TOKENS, D), jnp.bfloat16), hand_grad[:-1]], axis=0)
    return (next_grad, down_grad, gain_grad)
```

```python
import functools

import jax
import jax.numpy as jnp
from jax import lax
from jax.experimental import pallas as pl
from jax.experimental.pallas import tpu as pltpu
from jax.sharding import PartitionSpec as P

F32 = jnp.float32
BF16 = jnp.bfloat16
MESH = pl.DeviceIdType.MESH

HD = 128
NZ = 8
SH = 128
D = 2048
T = 2048
KC = 256
NKC = T // KC
QR = 32
EPS = 1e-6
FACTOR = HD**-0.5


def mul_t(a, b):
    return lax.dot_general(a, b, (((1,), (1,)), ((), ())), preferred_element_type=F32)


def mul(a, b):
    return jnp.dot(a, b, preferred_element_type=F32)


def kernel(
    nsec,
    go_ref,
    bi_ref,
    sk_ref,
    qkv_ref,
    wo_ref,
    wq_ref,
    gate_ref,
    scale_ref,
    gain_ref,
    next_ref,
    down_ref,
    gg_ref,
    go_v,
    bi_v,
    sk_v,
    qkv_v,
    w2,
    wcat,
    gath,
    sbuf,
    pbuf,
    obuf,
    kt,
    vt,
    vaug,
    gblk,
    gsend,
    dk_acc,
    dv_acc,
    xx,
    xpar,
    ybuf,
    rsend,
    rrecv,
    xhat,
    rstd_v,
    hand,
    down_v,
    gslots,
    ld_sem,
    ag_s,
    ag_r,
    wo_s,
    wo_r,
    wq_s,
    wq_r,
    g_s,
    g_r,
    x_s,
    x_r,
    rs_s,
    rs_r,
    nx_s,
    nx_r,
    dn_sem,
    gg_s,
    gg_r,
):
    sec = lax.axis_index("section")
    me = lax.axis_index("seq")
    z = lax.div(me, 2)
    y = lax.rem(me, 2)

    def zmod(v):
        return lax.rem(v + 2 * NZ, NZ)

    def dev(zz, yy):
        return (sec, zz * 2 + yy)

    z_to = (dev(zmod(z + 1), y), dev(zmod(z - 1), y))
    partner = dev(z, 1 - y)

    loads = [
        pltpu.make_async_copy(src, dst, ld_sem.at[i])
        for i, (src, dst) in enumerate(
            [
                (go_ref, go_v),
                (qkv_ref, qkv_v),
                (wo_ref, w2.at[pl.ds(0, SH)]),
                (wq_ref, wcat.at[pl.ds(0, 3)]),
                (bi_ref, bi_v),
                (sk_ref, sk_v),
            ]
        )
    ]
    for copy in loads:
        copy.start()

    barrier = pltpu.get_barrier_semaphore()

    @pl.loop(1, 2 * NZ)
    def _(off):
        pl.semaphore_signal(
            barrier, inc=1, device_id=(sec, lax.rem(me + off, 2 * NZ)), device_id_type=MESH
        )

    greeted = 2 * NZ - 1
    if nsec > 1:
        for step in (1, nsec - 1):
            pl.semaphore_signal(
                barrier, inc=1, device_id=(lax.rem(sec + step, nsec), me), device_id_type=MESH
            )
        greeted += 2

    loads[0].wait()
    gath[z] = (go_v[...].astype(F32) * gate_ref[...]).astype(BF16)
    pl.semaphore_wait(barrier, greeted)

    def ag_copy(way, pos, shard):
        half = lax.rem(pos, 2) if way == 0 else 1 - lax.rem(pos, 2)
        part = gath.at[shard, pl.ds(pl.multiple_of(half * (SH // 2), SH // 2), SH // 2)]
        return pltpu.make_async_remote_copy(
            src_ref=part,
            dst_ref=part,
            send_sem=ag_s.at[way, pos],
            recv_sem=ag_r.at[way, pos],
            device_id=z_to[way],
            device_id_type=MESH,
        )

    def ag_out(way, pos):
        back = lax.div(pos, 2)
        return ag_copy(way, pos, zmod(z - back) if way == 0 else zmod(z + back))

    def ag_in(way, pos):
        back = lax.div(pos, 2) + 1
        return ag_copy(way, pos, zmod(z - back) if way == 0 else zmod(z + back))

    for pos in (0, 1):
        for way in (0, 1):
            ag_out(way, jnp.int32(pos)).start()

    def forward(pos):
        for way in (0, 1):
            ag_in(way, pos).wait_recv()
            ag_out(way, pos + 2).start()

    wo_copy = pltpu.make_async_remote_copy(
        src_ref=wo_ref,
        dst_ref=w2.at[pl.ds(SH, SH)],
        send_sem=wo_s,
        recv_sem=wo_r,
        device_id=partner,
        device_id_type=MESH,
    )
    wo_copy.start()

    def wq_copy(i):
        which = lax.div(i, 2)
        rows = pl.ds(pl.multiple_of(lax.rem(i, 2) * 64, 64), 64)
        return pltpu.make_async_remote_copy(
            src_ref=wq_ref.at[which, rows],
            dst_ref=wcat.at[3 + which, rows],
            send_sem=wq_s.at[i],
            recv_sem=wq_r.at[i],
            device_id=partner,
            device_id_type=MESH,
        )

    loads[1].wait()
    lanes = lax.broadcasted_iota(jnp.int32, (KC, HD), 1)
    eye = (
        lax.broadcasted_iota(jnp.int32, (HD, HD), 0)
        == lax.broadcasted_iota(jnp.int32, (HD, HD), 1)
    ).astype(F32).astype(BF16)
    ones2 = (lanes < 2).astype(F32).astype(BF16)

    @pl.loop(0, NKC)
    def _(c):
        rows = pl.ds(pl.multiple_of(c * KC, KC), KC)
        kk = qkv_v[1, rows]
        vv = qkv_v[2, rows]
        kt[c] = mul_t(eye, kk).astype(BF16)
        vt[c] = mul_t(eye, vv).astype(BF16)
        vaug[rows, pl.ds(0, HD)] = vv
        vaug[rows, pl.ds(HD, HD)] = ones2

    def block_of(b):
        d = lax.div(b + 1, 2)
        odd = lax.rem(b, 2)
        far1 = (1 - odd) * lax.div(b + 6, 7)
        far2 = 1 - odd * (1 - lax.div(b, 7))
        return (zmod(z + d), far1), (zmod(z - d), far2)

    def token_rows(zz, far):
        shard = zz * 2 + lax.rem(y + far, 2)
        return pl.ds(pl.multiple_of(shard * SH, SH), SH)

    def queries(b):
        one, two = block_of(b)
        return jnp.concatenate([qkv_v[0, token_rows(*one)], qkv_v[0, token_rows(*two)]], axis=0)

    def softmax_block(b):
        qb = queries(b)

        def scores(c, top):
            rows = pl.ds(pl.multiple_of(c * KC, KC), KC)
            s = mul_t(qkv_v[1, rows], qb)
            sbuf[rows, :] = s
            return jnp.maximum(top, s.reshape(KC // 8, 8, 256).max(axis=0))

        top = lax.fori_loop(0, NKC, scores, jnp.full((8, 256), -jnp.inf, F32))
        top = jnp.max(top, axis=0, keepdims=True)

        def weights(c, total):
            rows = pl.ds(pl.multiple_of(c * KC, KC), KC)
            e = jnp.exp((sbuf[rows, :] - top) * FACTOR)
            sbuf[rows, :] = e
            return total + e.reshape(KC // 8, 8, 256).sum(axis=0)

        total = lax.fori_loop(0, NKC, weights, jnp.zeros((8, 256), F32))
        inverse = 1.0 / jnp.sum(total, axis=0, keepdims=True)

        def output(c, acc):
            rows = pl.ds(pl.multiple_of(c * KC, KC), KC)
            p = (sbuf[rows, :] * inverse).astype(BF16)
            pbuf[b, rows, :] = p
            return acc + mul(vt[c], p)

        out_t = lax.fori_loop(0, NKC, output, jnp.zeros((HD, 256), F32))
        obuf[b] = out_t.T

    dk_acc[...] = jnp.zeros_like(dk_acc)
    dv_acc[...] = jnp.zeros_like(dv_acc)

    def start_wq(i):
        wq_copy(jnp.int32(i)).start()

    @pl.loop(0, 3)
    def _(b):
        softmax_block(b)

    forward(jnp.int32(0))
    start_wq(0)

    @pl.loop(3, 8)
    def _(b):
        softmax_block(b)

    forward(jnp.int32(1))
    start_wq(1)

    def g_copy(d, two):
        if two:
            src, dst = gsend.at[d], gblk.at[2 * d]
        else:
            blk = 0 if d == 0 else 7
            src, dst = gsend.at[d, pl.ds(0, SH)], gblk.at[blk, pl.ds(SH, SH)]
        return pltpu.make_async_remote_copy(
            src_ref=src,
            dst_ref=dst,
            send_sem=g_s.at[d],
            recv_sem=g_r.at[d],
            device_id=partner,
            device_id_type=MESH,
        )

    def backward_block(b):
        qb = queries(b)
        g = gblk[b]
        delta = jnp.sum(g.astype(F32) * obuf[b], axis=1, keepdims=True)
        high = delta.astype(BF16).astype(F32)
        low = delta - high
        extra = jnp.where(lanes == 0, -high, jnp.where(lanes == 1, -low, 0.0)).astype(BF16)
        gaug = jnp.concatenate([g, extra], axis=1)

        def step(c, dq_t):
            rows = pl.ds(pl.multiple_of(c * KC, KC), KC)
            p = pbuf[b, rows, :]
            ds = (p.astype(F32) * mul_t(vaug[rows, :], gaug)).astype(BF16)
            dk_acc[rows, :] += mul(ds, qb)
            dv_acc[rows, :] += mul(p, g)
            return dq_t + mul(kt[c], ds)

        dq_t = lax.fori_loop(0, NKC, step, jnp.zeros((HD, 256), F32))
        dq = (dq_t.T * FACTOR).astype(BF16)
        one, two = block_of(b)
        xx[one[1], one[0], :, pl.ds(0, HD)] = dq[:SH]
        xx[two[1], two[0], :, pl.ds(0, HD)] = dq[SH:]

    loads[2].wait()
    wo_copy.wait_recv()

    def single(d):
        res = mul_t(gath[zmod(z + d)], w2[...]).astype(BF16)
        blk = 0 if d == 0 else 7
        gsend[d, pl.ds(0, SH)] = res[:, HD:]
        g_copy(d, False).start()
        gblk[blk, pl.ds(0, SH)] = res[:, :HD]
        g_copy(d, False).wait_recv()
        backward_block(jnp.int32(blk))

    single(0)

    def pair(d):
        both = jnp.concatenate([gath[zmod(z + d)], gath[zmod(z - d)]], axis=0)
        res = mul_t(both, w2[...]).astype(BF16)
        gsend[d] = res[:, HD:]
        g_copy(d, True).start()
        gblk[2 * d - 1] = res[:, :HD]
        backward_block(2 * d - 1)
        g_copy(d, True).wait_recv()
        backward_block(2 * d)

    @pl.loop(1, 4)
    def _(d):
        pair(d)
        wq_copy(d + 1).start()

        @pl.when(d == 1)
        def _():
            wq_copy(jnp.int32(5)).start()

        @pl.when(d < 3)
        def _():
            forward(2 * d)

        @pl.when(d == 1)
        def _():
            forward(jnp.int32(3))

        @pl.when(d == 2)
        def _():
            for way in (0, 1):
                ag_in(way, jnp.int32(5)).wait_recv()

        @pl.when(d == 3)
        def _():
            for way in (0, 1):
                ag_in(way, jnp.int32(6)).wait_recv()

    single(4)

    def x_copy(zz):
        return pltpu.make_async_remote_copy(
            src_ref=xx.at[1, zz],
            dst_ref=xpar.at[zz],
            send_sem=x_s.at[zz],
            recv_sem=x_r.at[zz],
            device_id=partner,
            device_id_type=MESH,
        )

    def place(zz, far):
        rows = token_rows(zz, far)
        xx[far, zz, :, pl.ds(HD, HD)] = (dk_acc[rows, :] * FACTOR).astype(BF16)
        xx[far, zz, :, pl.ds(2 * HD, HD)] = dv_acc[rows, :].astype(BF16)

    def in_order(i):
        away = 4 - lax.div(i + 1, 2)
        return zmod(z + away * (2 * lax.rem(i, 2) - 1))

    @pl.loop(0, NZ)
    def _(i):
        zz = in_order(i)
        place(zz, 1)
        x_copy(zz).start()

    @pl.loop(0, NZ)
    def _(i):
        place(in_order(i), 0)

    loads[3].wait()

    @pl.loop(0, 6)
    def _(i):
        wq_copy(i).wait_recv()

    def shard_x(zz):
        return jnp.concatenate([xx[0, zz], xpar[zz]], axis=1)

    def product(x, rows):
        @pl.loop(0, D // 512)
        def _(n):
            cols = pl.ds(pl.multiple_of(n * 512, 512), 512)
            w = wcat[:, :, cols].reshape(6 * HD, 512)
            ybuf[pl.ds(0, rows), cols] = mul(x, w)

    def rs_copy(way, pos):
        return pltpu.make_async_remote_copy(
            src_ref=rsend.at[way, pos],
            dst_ref=rrecv.at[way, pos],
            send_sem=rs_s.at[way, pos],
            recv_sem=rs_r.at[way, pos],
            device_id=z_to[way],
            device_id_type=MESH,
        )

    def piece(way, k):
        q = lax.rem(k, 2) if way else 1 - lax.rem(k, 2)
        return 2 * q + lax.div(k, 2)

    far4 = zmod(z + 4)
    x_copy(far4).wait_recv()
    product(shard_x(far4), SH)
    for k in (0, 1):
        for way in (0, 1):
            rsend[way, k] = ybuf[pl.ds((2 * way + k) * QR, QR), :].astype(BF16)
            rs_copy(way, k).start()

    loads[4].wait()
    loads[5].wait()

    @pl.loop(0, SH // QR)
    def _(i):
        rows = pl.ds(pl.multiple_of(i * QR, QR), QR)
        xv = bi_v[rows, :].astype(F32)
        centered = xv - jnp.mean(xv, axis=-1, keepdims=True)
        var = jnp.mean(centered * centered, axis=-1, keepdims=True)
        rstd = 1.0 / jnp.sqrt(var + EPS)
        xhat[rows, :] = centered * rstd
        rstd_v[rows, :] = jnp.broadcast_to(rstd, (QR, HD))

    def pair_product(d):
        plus, minus = zmod(z + d), zmod(z - d)
        x_copy(plus).wait_recv()
        x_copy(minus).wait_recv()
        product(jnp.concatenate([shard_x(plus), shard_x(minus)], axis=0), 2 * SH)

    def rows_of(way, k):
        return pl.ds(pl.multiple_of(way * SH + piece(way, k) * QR, QR), QR)

    def send_fresh(k):
        for way in (0, 1):
            rsend[way, 2 + k] = ybuf[rows_of(way, k), :].astype(BF16)
            rs_copy(way, 2 + k).start()

    def send_added(pos, k, came):
        for way in (0, 1):
            rs_copy(way, came).wait_recv()
            rsend[way, pos] = (ybuf[rows_of(way, k), :] + rrecv[way, came].astype(F32)).astype(BF16)
            rs_copy(way, pos).start()

    pair_product(3)
    for k in range(4):
        if k % 2 == 0:
            send_fresh(k)
        else:
            send_added(2 + k, k, k // 2)

    @pl.loop(1, 3)
    def _(s):
        pair_product(3 - s)

        @pl.loop(0, 4)
        def _(k):
            pos = 2 + 4 * s + k
            send_added(pos, k, pos - 4)

    x_copy(z).wait_recv()
    product(shard_x(z), SH)

    last = jnp.where(sec == nsec - 1, 1.0, 0.0).astype(F32)
    one_scale = 1.0 + scale_ref[...]
    down_gain = gain_ref[...] + last

    def next_copy(q):
        rows = pl.ds(pl.multiple_of(q * QR, QR), QR)
        return pltpu.make_async_remote_copy(
            src_ref=hand.at[rows],
            dst_ref=next_ref.at[rows],
            send_sem=nx_s.at[q],
            recv_sem=nx_r.at[q],
            device_id=(lax.rem(sec + 1, nsec), me),
            device_id_type=MESH,
        )

    def down_copy(q):
        rows = pl.ds(pl.multiple_of(q * QR, QR), QR)
        return pltpu.make_async_copy(down_v.at[rows], down_ref.at[rows], dn_sem.at[q])

    def finish(q, plus_pos, minus_pos):
        rows = pl.ds(pl.multiple_of(q * QR, QR), QR)
        normed = ybuf[rows, :] + rrecv[0, plus_pos].astype(F32) + rrecv[1, minus_pos].astype(F32)
        xh = xhat[rows, :]
        scaled = normed * one_scale
        mean1 = jnp.mean(scaled, axis=-1, keepdims=True)
        mean2 = jnp.mean(scaled * xh, axis=-1, keepdims=True)
        rstd = rstd_v[rows, pl.ds(0, 1)]
        ig = go_v[rows, :].astype(F32) + rstd * (scaled - mean1 - xh * mean2)
        hand[rows, :] = ig.astype(BF16)
        if nsec > 1:

            @pl.when(sec < nsec - 1)
            def _():
                next_copy(q).start()

        down_v[rows, :] = (down_gain * ig).astype(BF16)
        down_copy(q).start()
        return jnp.sum(ig * sk_v[rows, :].astype(F32), axis=0, keepdims=True)

    gain_sum = jnp.zeros((1, D), F32)
    for j in (0, 1):
        for k in (2 * j, 2 * j + 1):
            for way in (0, 1):
                rs_copy(way, jnp.int32(10 + k)).wait_recv()
        gain_sum += finish(jnp.int32(j), 10 + 2 * j + 1, 10 + 2 * j)
        gain_sum += finish(jnp.int32(2 + j), 10 + 2 * j, 10 + 2 * j + 1)

    gslots[me] = gain_sum

    def gain_copy(off):
        return pltpu.make_async_remote_copy(
            src_ref=gslots.at[me],
            dst_ref=gslots.at[me],
            send_sem=gg_s.at[off],
            recv_sem=gg_r.at[off],
            device_id=(sec, lax.rem(me + off, 2 * NZ)),
            device_id_type=MESH,
        )

    def gain_in(off):
        came = lax.rem(me - off + 2 * NZ, 2 * NZ)
        return pltpu.make_async_remote_copy(
            src_ref=gslots.at[came],
            dst_ref=gslots.at[came],
            send_sem=gg_s.at[off],
            recv_sem=gg_r.at[off],
            device_id=(sec, lax.rem(me + off, 2 * NZ)),
            device_id_type=MESH,
        )

    @pl.loop(1, 2 * NZ)
    def _(off):
        gain_copy(off).start()

    @pl.loop(0, 7)
    def _(pos):
        for way in (0, 1):
            ag_out(way, pos).wait_send()

    if nsec > 1:

        @pl.when(sec == 0)
        def _():
            gath[0] = jnp.zeros((SH, D), BF16)
            zero = pltpu.make_async_copy(gath.at[0], next_ref, nx_r.at[0])
            zero.start()
            zero.wait()

    @pl.loop(1, 2 * NZ)
    def _(off):
        gain_in(off).wait_recv()

    gg_ref[...] = jnp.sum(gslots[...], axis=0)

    wo_copy.wait_send()

    @pl.loop(0, 6)
    def _(i):
        wq_copy(i).wait_send()

    for d in range(5):
        g_copy(d, 0 < d < 4).wait_send()

    @pl.loop(0, NZ)
    def _(i):
        x_copy(i).wait_send()

    @pl.loop(0, 14)
    def _(pos):
        for way in (0, 1):
            rs_copy(way, pos).wait_send()

    @pl.loop(0, 4)
    def _(q):
        down_copy(q).wait()

    @pl.loop(1, 2 * NZ)
    def _(off):
        gain_copy(off).wait_send()

    if nsec > 1:

        @pl.when(sec < nsec - 1)
        def _():
            @pl.loop(0, 4)
            def _(q):
                next_copy(q).wait_send()

        @pl.when(sec > 0)
        def _():
            @pl.loop(0, 4)
            def _(q):
                next_copy(q).wait_recv()


def on_device(nsec, go, bi, sk, qkv, wo, wq, gate, scale, gain):
    any_spec = pl.BlockSpec(memory_space=pl.ANY)
    vmem_spec = pl.BlockSpec(memory_space=pltpu.VMEM)
    dma = pltpu.SemaphoreType.DMA
    nxt, down, gg = pl.pallas_call(
        functools.partial(kernel, nsec),
        out_shape=(
            jax.ShapeDtypeStruct((SH, D), BF16),
            jax.ShapeDtypeStruct((SH, D), BF16),
            jax.ShapeDtypeStruct((1, D), F32),
        ),
        in_specs=[any_spec] * 6 + [vmem_spec] * 3,
        out_specs=(any_spec, any_spec, vmem_spec),
        scratch_shapes=[
            pltpu.VMEM((SH, D), BF16),
            pltpu.VMEM((SH, D), BF16),
            pltpu.VMEM((SH, D), BF16),
            pltpu.VMEM((3, T, HD), BF16),
            pltpu.VMEM((2 * SH, D), BF16),
            pltpu.VMEM((6, HD, D), BF16),
            pltpu.VMEM((NZ, SH, D), BF16),
            pltpu.VMEM((T, 256), F32),
            pltpu.VMEM((8, T, 256), BF16),
            pltpu.VMEM((8, 256, HD), F32),
            pltpu.VMEM((NKC, HD, KC), BF16),
            pltpu.VMEM((NKC, HD, KC), BF16),
            pltpu.VMEM((T, 2 * HD), BF16),
            pltpu.VMEM((8, 256, HD), BF16),
            pltpu.VMEM((5, 256, HD), BF16),
            pltpu.VMEM((T, HD), F32),
            pltpu.VMEM((T, HD), F32),
            pltpu.VMEM((2, NZ, SH, 3 * HD), BF16),
            pltpu.VMEM((NZ, SH, 3 * HD), BF16),
            pltpu.VMEM((2 * SH, D), F32),
            pltpu.VMEM((2, 14, QR, D), BF16),
            pltpu.VMEM((2, 14, QR, D), BF16),
            pltpu.VMEM((SH, D), F32),
            pltpu.VMEM((SH, HD), F32),
            pltpu.VMEM((SH, D), BF16),
            pltpu.VMEM((SH, D), BF16),
            pltpu.VMEM((2 * NZ, 1, D), F32),
            dma((6,)),
            dma((2, 7)),
            dma((2, 7)),
            dma,
            dma,
            dma((6,)),
            dma((6,)),
            dma((5,)),
            dma((5,)),
            dma((NZ,)),
            dma((NZ,)),
            dma((2, 14)),
            dma((2, 14)),
            dma((4,)),
            dma((4,)),
            dma((4,)),
            dma((2 * NZ,)),
            dma((2 * NZ,)),
        ],
        compiler_params=pltpu.CompilerParams(
            collective_id=0, has_side_effects=True, vmem_limit_bytes=56 * 2**20
        ),
    )(go[0], bi[0], sk[0], qkv[0], wo[0], wq[0], gate, scale, gain)
    return nxt[None], down[None], gg


def solution(mesh):
    in_specs = (
        P("section", "seq", None),
        P("section", "seq", None),
        P("section", "seq", None),
        P("section", None, None, "seq"),
        P("section", "seq", None),
        P("section", None, "seq", None),
        P("section", None),
        P("section", None),
        P("section", None),
    )
    out_specs = (P("section", "seq", None), P("section", "seq", None), P("section", None))
    return jax.shard_map(
        functools.partial(on_device, mesh.shape["section"]),
        mesh=mesh,
        in_specs=in_specs,
        out_specs=out_specs,
        check_vma=False,
    )
```

```python
import functools

import jax
import jax.numpy as jnp
from jax import lax
from jax.experimental import pallas as pl
from jax.experimental.pallas import tpu as pltpu
from jax.sharding import PartitionSpec as P

F32 = jnp.float32
BF16 = jnp.bfloat16
MESH = pl.DeviceIdType.MESH

HD = 128
NZ = 8
SH = 128
D = 2048
T = 2048
KC = 256
NKC = T // KC
UN = 8
QR = 32
EPS = 1e-6
FACTOR = HD**-0.5


def mul_t(a, b):
    return lax.dot_general(a, b, (((1,), (1,)), ((), ())), preferred_element_type=F32)


def mul(a, b):
    return jnp.dot(a, b, preferred_element_type=F32)


def kernel(
    nsec,
    go_ref,
    bi_ref,
    sk_ref,
    qkv_ref,
    wo_ref,
    wq_ref,
    gate_ref,
    scale_ref,
    gain_ref,
    next_ref,
    down_ref,
    gg_ref,
    go_v,
    bi_v,
    sk_v,
    qkv_v,
    w2,
    wcat,
    gath,
    sbuf,
    pbuf,
    obuf,
    kt,
    vt,
    vaug,
    gblk,
    gsend,
    dk_acc,
    dv_acc,
    xx,
    xpar,
    ybuf,
    rsend,
    rrecv,
    xhat,
    rstd_v,
    hand,
    down_v,
    gslots,
    ld_sem,
    ag_s,
    ag_r,
    wo_s,
    wo_r,
    wq_s,
    wq_r,
    g_s,
    g_r,
    x_s,
    x_r,
    rs_s,
    rs_r,
    nx_s,
    nx_r,
    dn_sem,
    gg_s,
    gg_r,
):
    sec = lax.axis_index("section")
    me = lax.axis_index("seq")
    z = lax.div(me, 2)
    y = lax.rem(me, 2)

    def zmod(v):
        return lax.rem(v + 2 * NZ, NZ)

    def dev(zz, yy):
        return (sec, zz * 2 + yy)

    z_to = (dev(zmod(z + 1), y), dev(zmod(z - 1), y))
    partner = dev(z, 1 - y)

    loads = [
        pltpu.make_async_copy(src, dst, ld_sem.at[i])
        for i, (src, dst) in enumerate(
            [
                (go_ref, go_v),
                (qkv_ref, qkv_v),
                (wo_ref, w2.at[pl.ds(0, SH)]),
                (wq_ref, wcat.at[pl.ds(0, 3)]),
                (bi_ref, bi_v),
                (sk_ref, sk_v),
            ]
        )
    ]
    for copy in loads:
        copy.start()

    barrier = pltpu.get_barrier_semaphore()

    @pl.loop(1, 2 * NZ)
    def _(off):
        pl.semaphore_signal(
            barrier, inc=1, device_id=(sec, lax.rem(me + off, 2 * NZ)), device_id_type=MESH
        )

    greeted = 2 * NZ - 1
    if nsec > 1:
        for step in (1, nsec - 1):
            pl.semaphore_signal(
                barrier, inc=1, device_id=(lax.rem(sec + step, nsec), me), device_id_type=MESH
            )
        greeted += 2

    loads[0].wait()
    gath[z] = (go_v[...].astype(F32) * gate_ref[...]).astype(BF16)
    pl.semaphore_wait(barrier, greeted)

    def ag_copy(way, pos, shard):
        half = lax.rem(pos, 2) if way == 0 else 1 - lax.rem(pos, 2)
        part = gath.at[shard, pl.ds(pl.multiple_of(half * (SH // 2), SH // 2), SH // 2)]
        return pltpu.make_async_remote_copy(
            src_ref=part,
            dst_ref=part,
            send_sem=ag_s.at[way, pos],
            recv_sem=ag_r.at[way, pos],
            device_id=z_to[way],
            device_id_type=MESH,
        )

    def ag_out(way, pos):
        back = lax.div(pos, 2)
        return ag_copy(way, pos, zmod(z - back) if way == 0 else zmod(z + back))

    def ag_in(way, pos):
        back = lax.div(pos, 2) + 1
        return ag_copy(way, pos, zmod(z - back) if way == 0 else zmod(z + back))

    for pos in (0, 1):
        for way in (0, 1):
            ag_out(way, jnp.int32(pos)).start()

    def forward(pos):
        for way in (0, 1):
            ag_in(way, pos).wait_recv()
            ag_out(way, pos + 2).start()
        wq_copy(pos).start()

    wo_copy = pltpu.make_async_remote_copy(
        src_ref=wo_ref,
        dst_ref=w2.at[pl.ds(SH, SH)],
        send_sem=wo_s,
        recv_sem=wo_r,
        device_id=partner,
        device_id_type=MESH,
    )
    wo_copy.start()

    def wq_copy(i):
        which = lax.div(i, 2)
        rows = pl.ds(pl.multiple_of(lax.rem(i, 2) * 64, 64), 64)
        return pltpu.make_async_remote_copy(
            src_ref=wq_ref.at[which, rows],
            dst_ref=wcat.at[3 + which, rows],
            send_sem=wq_s.at[i],
            recv_sem=wq_r.at[i],
            device_id=partner,
            device_id_type=MESH,
        )

    loads[1].wait()
    lanes = lax.broadcasted_iota(jnp.int32, (KC, HD), 1)
    eye = (
        lax.broadcasted_iota(jnp.int32, (HD, HD), 0)
        == lax.broadcasted_iota(jnp.int32, (HD, HD), 1)
    ).astype(F32).astype(BF16)
    ones2 = (lanes < 2).astype(F32).astype(BF16)

    @pl.loop(0, NKC)
    def _(c):
        rows = pl.ds(pl.multiple_of(c * KC, KC), KC)
        kk = qkv_v[1, rows]
        vv = qkv_v[2, rows]
        kt[c] = mul_t(eye, kk).astype(BF16)
        vt[c] = mul_t(eye, vv).astype(BF16)
        vaug[rows, pl.ds(0, HD)] = vv
        vaug[rows, pl.ds(HD, HD)] = ones2

    def block_of(b):
        d = lax.div(b + 1, 2)
        odd = lax.rem(b, 2)
        far1 = (1 - odd) * lax.div(b + 6, 7)
        far2 = 1 - odd * (1 - lax.div(b, 7))
        return (zmod(z + d), far1), (zmod(z - d), far2)

    def token_rows(zz, far):
        shard = zz * 2 + lax.rem(y + far, 2)
        return pl.ds(pl.multiple_of(shard * SH, SH), SH)

    def queries(b):
        one, two = block_of(b)
        return jnp.concatenate([qkv_v[0, token_rows(*one)], qkv_v[0, token_rows(*two)]], axis=0)

    def softmax_block(b):
        qb = queries(b)

        def scores(c, top):
            rows = pl.ds(pl.multiple_of(c * KC, KC), KC)
            s = mul_t(qkv_v[1, rows], qb)
            sbuf[rows, :] = s
            return jnp.maximum(top, s.reshape(KC // 8, 8, 256).max(axis=0))

        top = lax.fori_loop(0, NKC, scores, jnp.full((8, 256), -jnp.inf, F32), unroll=UN)
        top = jnp.max(top, axis=0, keepdims=True)

        def weights(c, total):
            rows = pl.ds(pl.multiple_of(c * KC, KC), KC)
            e = jnp.exp((sbuf[rows, :] - top) * FACTOR)
            sbuf[rows, :] = e
            return total + e.reshape(KC // 8, 8, 256).sum(axis=0)

        total = lax.fori_loop(0, NKC, weights, jnp.zeros((8, 256), F32), unroll=UN)
        inverse = 1.0 / jnp.sum(total, axis=0, keepdims=True)

        def output(c, acc):
            rows = pl.ds(pl.multiple_of(c * KC, KC), KC)
            p = (sbuf[rows, :] * inverse).astype(BF16)
            pbuf[b, rows, :] = p
            return acc + mul(vt[c], p)

        out_t = lax.fori_loop(0, NKC, output, jnp.zeros((HD, 256), F32), unroll=UN)
        obuf[b] = out_t.T

    dk_acc[...] = jnp.zeros_like(dk_acc)
    dv_acc[...] = jnp.zeros_like(dv_acc)

    @pl.loop(0, 8)
    def _(b):
        softmax_block(b)

        @pl.when(lax.rem(b, 3) == 2)
        def _():
            forward(lax.div(b, 3))

    def g_copy(d, two):
        if two:
            src, dst = gsend.at[d], gblk.at[2 * d]
        else:
            blk = 0 if d == 0 else 7
            src, dst = gsend.at[d, pl.ds(0, SH)], gblk.at[blk, pl.ds(SH, SH)]
        return pltpu.make_async_remote_copy(
            src_ref=src,
            dst_ref=dst,
            send_sem=g_s.at[d],
            recv_sem=g_r.at[d],
            device_id=partner,
            device_id_type=MESH,
        )

    def backward_block(b):
        qb = queries(b)
        g = gblk[b]
        delta = jnp.sum(g.astype(F32) * obuf[b], axis=1, keepdims=True)
        high = delta.astype(BF16).astype(F32)
        low = delta - high
        extra = jnp.where(lanes == 0, -high, jnp.where(lanes == 1, -low, 0.0)).astype(BF16)
        gaug = jnp.concatenate([g, extra], axis=1)

        def step(c, dq_t):
            rows = pl.ds(pl.multiple_of(c * KC, KC), KC)
            p = pbuf[b, rows, :]
            ds = (p.astype(F32) * mul_t(vaug[rows, :], gaug)).astype(BF16)
            dk_acc[rows, :] += mul(ds, qb)
            dv_acc[rows, :] += mul(p, g)
            return dq_t + mul(kt[c], ds)

        dq_t = lax.fori_loop(0, NKC, step, jnp.zeros((HD, 256), F32), unroll=UN)
        dq = (dq_t.T * FACTOR).astype(BF16)
        one, two = block_of(b)
        xx[one[1], one[0], :, pl.ds(0, HD)] = dq[:SH]
        xx[two[1], two[0], :, pl.ds(0, HD)] = dq[SH:]

    loads[2].wait()
    wo_copy.wait_recv()

    def single(d):
        res = mul_t(gath[zmod(z + d)], w2[...]).astype(BF16)
        blk = 0 if d == 0 else 7
        gsend[d, pl.ds(0, SH)] = res[:, HD:]
        g_copy(d, False).start()
        gblk[blk, pl.ds(0, SH)] = res[:, :HD]
        g_copy(d, False).wait_recv()
        backward_block(jnp.int32(blk))

    single(0)

    def pair(d):
        both = jnp.concatenate([gath[zmod(z + d)], gath[zmod(z - d)]], axis=0)
        res = mul_t(both, w2[...]).astype(BF16)
        gsend[d] = res[:, HD:]
        g_copy(d, True).start()
        gblk[2 * d - 1] = res[:, :HD]
        backward_block(2 * d - 1)
        g_copy(d, True).wait_recv()
        backward_block(2 * d)

    forward(jnp.int32(2))

    @pl.loop(1, 4)
    def _(d):
        pair(d)

        @pl.when(d < 3)
        def _():
            forward(d + 2)

        @pl.when(d > 1)
        def _():
            for way in (0, 1):
                ag_in(way, d + 3).wait_recv()

        @pl.when(d == 2)
        def _():
            wq_copy(jnp.int32(5)).start()

    single(4)

    def x_copy(zz):
        return pltpu.make_async_remote_copy(
            src_ref=xx.at[1, zz],
            dst_ref=xpar.at[zz],
            send_sem=x_s.at[zz],
            recv_sem=x_r.at[zz],
            device_id=partner,
            device_id_type=MESH,
        )

    def place(zz, far):
        rows = token_rows(zz, far)
        xx[far, zz, :, pl.ds(HD, HD)] = (dk_acc[rows, :] * FACTOR).astype(BF16)
        xx[far, zz, :, pl.ds(2 * HD, HD)] = dv_acc[rows, :].astype(BF16)

    def in_order(i):
        away = 4 - lax.div(i + 1, 2)
        return zmod(z + away * (2 * lax.rem(i, 2) - 1))

    place(in_order(jnp.int32(0)), 1)
    x_copy(in_order(jnp.int32(0))).start()

    @pl.loop(1, NZ)
    def _(i):
        place(in_order(i), 1)

    def start_x(i):
        x_copy(in_order(jnp.int32(i))).start()

    start_x(1)
    start_x(2)

    @pl.loop(0, NZ)
    def _(i):
        place(in_order(i), 0)

    loads[3].wait()

    @pl.loop(0, 6)
    def _(i):
        wq_copy(i).wait_recv()

    def shard_x(zz):
        return jnp.concatenate([xx[0, zz], xpar[zz]], axis=1)

    def product(x, rows):
        @pl.loop(0, D // 512)
        def _(n):
            cols = pl.ds(pl.multiple_of(n * 512, 512), 512)
            w = wcat[:, :, cols].reshape(6 * HD, 512)
            ybuf[pl.ds(0, rows), cols] = mul(x, w)

    def rs_copy(way, pos):
        return pltpu.make_async_remote_copy(
            src_ref=rsend.at[way, pos],
            dst_ref=rrecv.at[way, pos],
            send_sem=rs_s.at[way, pos],
            recv_sem=rs_r.at[way, pos],
            device_id=z_to[way],
            device_id_type=MESH,
        )

    def piece(way, k):
        q = lax.rem(k, 2) if way else 1 - lax.rem(k, 2)
        return 2 * q + lax.div(k, 2)

    far4 = zmod(z + 4)
    x_copy(far4).wait_recv()
    start_x(3)
    start_x(4)
    product(shard_x(far4), SH)
    for k in (0, 1):
        for way in (0, 1):
            rsend[way, k] = ybuf[pl.ds((2 * way + k) * QR, QR), :].astype(BF16)
            rs_copy(way, k).start()

    loads[4].wait()
    loads[5].wait()

    @pl.loop(0, SH // QR)
    def _(i):
        rows = pl.ds(pl.multiple_of(i * QR, QR), QR)
        xv = bi_v[rows, :].astype(F32)
        centered = xv - jnp.mean(xv, axis=-1, keepdims=True)
        var = jnp.mean(centered * centered, axis=-1, keepdims=True)
        rstd = 1.0 / jnp.sqrt(var + EPS)
        xhat[rows, :] = centered * rstd
        rstd_v[rows, :] = jnp.broadcast_to(rstd, (QR, HD))

    def pair_product(d):
        plus, minus = zmod(z + d), zmod(z - d)
        x_copy(plus).wait_recv()
        x_copy(minus).wait_recv()

        @pl.when(d == 3)
        def _():
            start_x(5)
            start_x(6)

        @pl.when(d == 2)
        def _():
            start_x(7)

        product(jnp.concatenate([shard_x(plus), shard_x(minus)], axis=0), 2 * SH)

    def rows_of(way, k):
        return pl.ds(pl.multiple_of(way * SH + piece(way, k) * QR, QR), QR)

    def send_fresh(k):
        for way in (0, 1):
            rsend[way, 2 + k] = ybuf[rows_of(way, k), :].astype(BF16)
            rs_copy(way, 2 + k).start()

    def send_added(pos, k, came):
        for way in (0, 1):
            rs_copy(way, came).wait_recv()
            rsend[way, pos] = (ybuf[rows_of(way, k), :] + rrecv[way, came].astype(F32)).astype(BF16)
            rs_copy(way, pos).start()

    pair_product(jnp.int32(3))
    for k in range(4):
        if k % 2 == 0:
            send_fresh(k)
        else:
            send_added(2 + k, k, k // 2)

    @pl.loop(1, 3)
    def _(s):
        pair_product(3 - s)

        @pl.loop(0, 4)
        def _(k):
            pos = 2 + 4 * s + k
            send_added(pos, k, pos - 4)

    x_copy(z).wait_recv()
    product(shard_x(z), SH)

    last = jnp.where(sec == nsec - 1, 1.0, 0.0).astype(F32)
    one_scale = 1.0 + scale_ref[...]
    down_gain = gain_ref[...] + last

    def next_copy(q):
        rows = pl.ds(pl.multiple_of(q * QR, QR), QR)
        return pltpu.make_async_remote_copy(
            src_ref=hand.at[rows],
            dst_ref=next_ref.at[rows],
            send_sem=nx_s.at[q],
            recv_sem=nx_r.at[q],
            device_id=(lax.rem(sec + 1, nsec), me),
            device_id_type=MESH,
        )

    def down_copy(q):
        rows = pl.ds(pl.multiple_of(q * QR, QR), QR)
        return pltpu.make_async_copy(down_v.at[rows], down_ref.at[rows], dn_sem.at[q])

    def finish(q, plus_pos, minus_pos):
        rows = pl.ds(pl.multiple_of(q * QR, QR), QR)
        normed = ybuf[rows, :] + rrecv[0, plus_pos].astype(F32) + rrecv[1, minus_pos].astype(F32)
        xh = xhat[rows, :]
        scaled = normed * one_scale
        mean1 = jnp.mean(scaled, axis=-1, keepdims=True)
        mean2 = jnp.mean(scaled * xh, axis=-1, keepdims=True)
        rstd = rstd_v[rows, pl.ds(0, 1)]
        ig = go_v[rows, :].astype(F32) + rstd * (scaled - mean1 - xh * mean2)
        hand[rows, :] = ig.astype(BF16)
        if nsec > 1:

            @pl.when(sec < nsec - 1)
            def _():
                next_copy(q).start()

        down_v[rows, :] = (down_gain * ig).astype(BF16)
        down_copy(q).start()
        return jnp.sum(ig * sk_v[rows, :].astype(F32), axis=0, keepdims=True)

    gain_sum = jnp.zeros((1, D), F32)
    for j in (0, 1):
        for k in (2 * j, 2 * j + 1):
            for way in (0, 1):
                rs_copy(way, jnp.int32(10 + k)).wait_recv()
        gain_sum += finish(jnp.int32(j), 10 + 2 * j + 1, 10 + 2 * j)
        gain_sum += finish(jnp.int32(2 + j), 10 + 2 * j, 10 + 2 * j + 1)

    gslots[me] = gain_sum

    def gain_copy(off):
        return pltpu.make_async_remote_copy(
            src_ref=gslots.at[me],
            dst_ref=gslots.at[me],
            send_sem=gg_s.at[off],
            recv_sem=gg_r.at[off],
            device_id=(sec, lax.rem(me + off, 2 * NZ)),
            device_id_type=MESH,
        )

    def gain_in(off):
        came = lax.rem(me - off + 2 * NZ, 2 * NZ)
        return pltpu.make_async_remote_copy(
            src_ref=gslots.at[came],
            dst_ref=gslots.at[came],
            send_sem=gg_s.at[off],
            recv_sem=gg_r.at[off],
            device_id=(sec, lax.rem(me + off, 2 * NZ)),
            device_id_type=MESH,
        )

    @pl.loop(1, 2 * NZ)
    def _(off):
        gain_copy(off).start()

    @pl.loop(0, 7)
    def _(pos):
        for way in (0, 1):
            ag_out(way, pos).wait_send()

    if nsec > 1:

        @pl.when(sec == 0)
        def _():
            gath[0] = jnp.zeros((SH, D), BF16)
            zero = pltpu.make_async_copy(gath.at[0], next_ref, nx_r.at[0])
            zero.start()
            zero.wait()

    @pl.loop(1, 2 * NZ)
    def _(off):
        gain_in(off).wait_recv()

    gg_ref[...] = jnp.sum(gslots[...], axis=0)

    wo_copy.wait_send()

    @pl.loop(0, 6)
    def _(i):
        wq_copy(i).wait_send()

    for d in range(5):
        g_copy(d, 0 < d < 4).wait_send()

    @pl.loop(0, NZ)
    def _(i):
        x_copy(i).wait_send()

    @pl.loop(0, 14)
    def _(pos):
        for way in (0, 1):
            rs_copy(way, pos).wait_send()

    @pl.loop(0, 4)
    def _(q):
        down_copy(q).wait()

    @pl.loop(1, 2 * NZ)
    def _(off):
        gain_copy(off).wait_send()

    if nsec > 1:

        @pl.when(sec < nsec - 1)
        def _():
            @pl.loop(0, 4)
            def _(q):
                next_copy(q).wait_send()

        @pl.when(sec > 0)
        def _():
            @pl.loop(0, 4)
            def _(q):
                next_copy(q).wait_recv()


def on_device(nsec, go, bi, sk, qkv, wo, wq, gate, scale, gain):
    any_spec = pl.BlockSpec(memory_space=pl.ANY)
    vmem_spec = pl.BlockSpec(memory_space=pltpu.VMEM)
    dma = pltpu.SemaphoreType.DMA
    nxt, down, gg = pl.pallas_call(
        functools.partial(kernel, nsec),
        out_shape=(
            jax.ShapeDtypeStruct((SH, D), BF16),
            jax.ShapeDtypeStruct((SH, D), BF16),
            jax.ShapeDtypeStruct((1, D), F32),
        ),
        in_specs=[any_spec] * 6 + [vmem_spec] * 3,
        out_specs=(any_spec, any_spec, vmem_spec),
        scratch_shapes=[
            pltpu.VMEM((SH, D), BF16),
            pltpu.VMEM((SH, D), BF16),
            pltpu.VMEM((SH, D), BF16),
            pltpu.VMEM((3, T, HD), BF16),
            pltpu.VMEM((2 * SH, D), BF16),
            pltpu.VMEM((6, HD, D), BF16),
            pltpu.VMEM((NZ, SH, D), BF16),
            pltpu.VMEM((T, 256), F32),
            pltpu.VMEM((8, T, 256), BF16),
            pltpu.VMEM((8, 256, HD), F32),
            pltpu.VMEM((NKC, HD, KC), BF16),
            pltpu.VMEM((NKC, HD, KC), BF16),
            pltpu.VMEM((T, 2 * HD), BF16),
            pltpu.VMEM((8, 256, HD), BF16),
            pltpu.VMEM((5, 256, HD), BF16),
            pltpu.VMEM((T, HD), F32),
            pltpu.VMEM((T, HD), F32),
            pltpu.VMEM((2, NZ, SH, 3 * HD), BF16),
            pltpu.VMEM((NZ, SH, 3 * HD), BF16),
            pltpu.VMEM((2 * SH, D), F32),
            pltpu.VMEM((2, 14, QR, D), BF16),
            pltpu.VMEM((2, 14, QR, D), BF16),
            pltpu.VMEM((SH, D), F32),
            pltpu.VMEM((SH, HD), F32),
            pltpu.VMEM((SH, D), BF16),
            pltpu.VMEM((SH, D), BF16),
            pltpu.VMEM((2 * NZ, 1, D), F32),
            dma((6,)),
            dma((2, 7)),
            dma((2, 7)),
            dma,
            dma,
            dma((6,)),
            dma((6,)),
            dma((5,)),
            dma((5,)),
            dma((NZ,)),
            dma((NZ,)),
            dma((2, 14)),
            dma((2, 14)),
            dma((4,)),
            dma((4,)),
            dma((4,)),
            dma((2 * NZ,)),
            dma((2 * NZ,)),
        ],
        compiler_params=pltpu.CompilerParams(
            collective_id=0, has_side_effects=True, vmem_limit_bytes=56 * 2**20
        ),
    )(go[0], bi[0], sk[0], qkv[0], wo[0], wq[0], gate, scale, gain)
    return nxt[None], down[None], gg


def solution(mesh):
    in_specs = (
        P("section", "seq", None),
        P("section", "seq", None),
        P("section", "seq", None),
        P("section", None, None, "seq"),
        P("section", "seq", None),
        P("section", None, "seq", None),
        P("section", None),
        P("section", None),
        P("section", None),
    )
    out_specs = (P("section", "seq", None), P("section", "seq", None), P("section", None))
    return jax.shard_map(
        functools.partial(on_device, mesh.shape["section"]),
        mesh=mesh,
        in_specs=in_specs,
        out_specs=out_specs,
        check_vma=False,
    )
```

```python
import functools

import jax
import jax.numpy as jnp
from jax import lax
from jax.experimental import pallas as pl
from jax.experimental.pallas import tpu as pltpu
from jax.sharding import PartitionSpec as P

F32 = jnp.float32
BF16 = jnp.bfloat16
MESH = pl.DeviceIdType.MESH

HD = 128
NZ = 8
SH = 128
D = 2048
T = 2048
KC = 256
NKC = T // KC
UN = 8
QR = 32
EPS = 1e-6
FACTOR = HD**-0.5


def mul_t(a, b):
    return lax.dot_general(a, b, (((1,), (1,)), ((), ())), preferred_element_type=F32)


def mul(a, b):
    return jnp.dot(a, b, preferred_element_type=F32)


def kernel(
    nsec,
    go_ref,
    bi_ref,
    sk_ref,
    qkv_ref,
    wo_ref,
    wq_ref,
    gate_ref,
    scale_ref,
    next_ref,
    ig_ref,
    gg_ref,
    go_v,
    bi_v,
    sk_v,
    qkv_v,
    w2,
    wcat,
    gath,
    sbuf,
    pbuf,
    obuf,
    kt,
    vt,
    vaug,
    gblk,
    gsend,
    dk_acc,
    dv_acc,
    xx,
    xpar,
    ybuf,
    rsend,
    rrecv,
    xhat,
    rstd_v,
    hand,
    ig_v,
    gslots,
    ld_sem,
    ag_s,
    ag_r,
    wo_s,
    wo_r,
    wq_s,
    wq_r,
    g_s,
    g_r,
    x_s,
    x_r,
    rs_s,
    rs_r,
    nx_s,
    nx_r,
    ig_sem,
    gg_s,
    gg_r,
):
    sec = lax.axis_index("section")
    me = lax.axis_index("seq")
    z = lax.div(me, 2)
    y = lax.rem(me, 2)

    def zmod(v):
        return lax.rem(v + 2 * NZ, NZ)

    def dev(zz, yy):
        return (sec, zz * 2 + yy)

    z_to = (dev(zmod(z + 1), y), dev(zmod(z - 1), y))
    partner = dev(z, 1 - y)

    loads = [
        pltpu.make_async_copy(src, dst, ld_sem.at[i])
        for i, (src, dst) in enumerate(
            [
                (go_ref, go_v),
                (qkv_ref, qkv_v),
                (wo_ref, w2.at[pl.ds(0, SH)]),
                (wq_ref, wcat.at[pl.ds(0, 3)]),
                (bi_ref, bi_v),
                (sk_ref, sk_v),
            ]
        )
    ]
    for copy in loads:
        copy.start()

    barrier = pltpu.get_barrier_semaphore()

    @pl.loop(1, 2 * NZ)
    def _(off):
        pl.semaphore_signal(
            barrier, inc=1, device_id=(sec, lax.rem(me + off, 2 * NZ)), device_id_type=MESH
        )

    greeted = 2 * NZ - 1
    if nsec > 1:
        for step in (1, nsec - 1):
            pl.semaphore_signal(
                barrier, inc=1, device_id=(lax.rem(sec + step, nsec), me), device_id_type=MESH
            )
        greeted += 2

    loads[0].wait()
    gath[z] = (go_v[...].astype(F32) * gate_ref[...]).astype(BF16)
    pl.semaphore_wait(barrier, greeted)

    def ag_copy(way, pos, shard):
        half = lax.rem(pos, 2) if way == 0 else 1 - lax.rem(pos, 2)
        part = gath.at[shard, pl.ds(pl.multiple_of(half * (SH // 2), SH // 2), SH // 2)]
        return pltpu.make_async_remote_copy(
            src_ref=part,
            dst_ref=part,
            send_sem=ag_s.at[way, pos],
            recv_sem=ag_r.at[way, pos],
            device_id=z_to[way],
            device_id_type=MESH,
        )

    def ag_out(way, pos):
        back = lax.div(pos, 2)
        return ag_copy(way, pos, zmod(z - back) if way == 0 else zmod(z + back))

    def ag_in(way, pos):
        back = lax.div(pos, 2) + 1
        return ag_copy(way, pos, zmod(z - back) if way == 0 else zmod(z + back))

    for pos in (0, 1):
        for way in (0, 1):
            ag_out(way, jnp.int32(pos)).start()

    def forward(pos):
        for way in (0, 1):
            ag_in(way, pos).wait_recv()
            ag_out(way, pos + 2).start()

    wo_copy = pltpu.make_async_remote_copy(
        src_ref=wo_ref,
        dst_ref=w2.at[pl.ds(SH, SH)],
        send_sem=wo_s,
        recv_sem=wo_r,
        device_id=partner,
        device_id_type=MESH,
    )
    wo_copy.start()

    def wq_copy(i):
        which = lax.div(i, 4)
        rows = pl.ds(pl.multiple_of(lax.rem(i, 4) * 32, 32), 32)
        return pltpu.make_async_remote_copy(
            src_ref=wq_ref.at[which, rows],
            dst_ref=wcat.at[3 + which, rows],
            send_sem=wq_s.at[i],
            recv_sem=wq_r.at[i],
            device_id=partner,
            device_id_type=MESH,
        )

    loads[1].wait()
    lanes = lax.broadcasted_iota(jnp.int32, (KC, HD), 1)
    eye = (
        lax.broadcasted_iota(jnp.int32, (HD, HD), 0)
        == lax.broadcasted_iota(jnp.int32, (HD, HD), 1)
    ).astype(F32).astype(BF16)
    ones2 = (lanes < 2).astype(F32).astype(BF16)

    @pl.loop(0, NKC)
    def _(c):
        rows = pl.ds(pl.multiple_of(c * KC, KC), KC)
        kk = qkv_v[1, rows]
        vv = qkv_v[2, rows]
        kt[c] = mul_t(eye, kk).astype(BF16)
        vt[c] = mul_t(eye, vv).astype(BF16)
        vaug[rows, pl.ds(0, HD)] = vv
        vaug[rows, pl.ds(HD, HD)] = ones2

    def block_of(b):
        d = lax.div(b + 1, 2)
        odd = lax.rem(b, 2)
        far1 = (1 - odd) * lax.div(b + 6, 7)
        far2 = 1 - odd * (1 - lax.div(b, 7))
        return (zmod(z + d), far1), (zmod(z - d), far2)

    def token_rows(zz, far):
        shard = zz * 2 + lax.rem(y + far, 2)
        return pl.ds(pl.multiple_of(shard * SH, SH), SH)

    def queries(b):
        one, two = block_of(b)
        return jnp.concatenate([qkv_v[0, token_rows(*one)], qkv_v[0, token_rows(*two)]], axis=0)

    def softmax_block(b):
        qb = queries(b)

        def scores(c, top):
            rows = pl.ds(pl.multiple_of(c * KC, KC), KC)
            s = mul_t(qkv_v[1, rows], qb)
            sbuf[rows, :] = s
            return jnp.maximum(top, s.reshape(KC // 8, 8, 256).max(axis=0))

        top = lax.fori_loop(0, NKC, scores, jnp.full((8, 256), -jnp.inf, F32), unroll=UN)
        top = jnp.max(top, axis=0, keepdims=True)

        def weights(c, total):
            rows = pl.ds(pl.multiple_of(c * KC, KC), KC)
            e = jnp.exp((sbuf[rows, :] - top) * FACTOR)
            sbuf[rows, :] = e
            return total + e.reshape(KC // 8, 8, 256).sum(axis=0)

        total = lax.fori_loop(0, NKC, weights, jnp.zeros((8, 256), F32), unroll=UN)
        inverse = 1.0 / jnp.sum(total, axis=0, keepdims=True)

        def output(c, acc):
            rows = pl.ds(pl.multiple_of(c * KC, KC), KC)
            p = (sbuf[rows, :] * inverse).astype(BF16)
            pbuf[b, rows, :] = p
            return acc + mul(vt[c], p)

        out_t = lax.fori_loop(0, NKC, output, jnp.zeros((HD, 256), F32), unroll=UN)
        obuf[b] = out_t.T

    dk_acc[...] = jnp.zeros_like(dk_acc)
    dv_acc[...] = jnp.zeros_like(dv_acc)

    @pl.loop(0, 8)
    def _(b):
        softmax_block(b)

        @pl.when(lax.rem(b, 3) == 2)
        def _():
            forward(lax.div(b, 3))

        @pl.when(b > 3)
        def _():
            wq_copy(b - 4).start()

    def g_copy(d, two):
        if two:
            src, dst = gsend.at[d], gblk.at[2 * d]
        else:
            blk = 0 if d == 0 else 7
            src, dst = gsend.at[d, pl.ds(0, SH)], gblk.at[blk, pl.ds(SH, SH)]
        return pltpu.make_async_remote_copy(
            src_ref=src,
            dst_ref=dst,
            send_sem=g_s.at[d],
            recv_sem=g_r.at[d],
            device_id=partner,
            device_id_type=MESH,
        )

    def backward_block(b):
        qb = queries(b)
        g = gblk[b]
        delta = jnp.sum(g.astype(F32) * obuf[b], axis=1, keepdims=True)
        high = delta.astype(BF16).astype(F32)
        low = delta - high
        extra = jnp.where(lanes == 0, -high, jnp.where(lanes == 1, -low, 0.0)).astype(BF16)
        gaug = jnp.concatenate([g, extra], axis=1)

        def step(c, dq_t):
            rows = pl.ds(pl.multiple_of(c * KC, KC), KC)
            p = pbuf[b, rows, :]
            ds = (p.astype(F32) * mul_t(vaug[rows, :], gaug)).astype(BF16)
            dk_acc[rows, :] += mul(ds, qb)
            dv_acc[rows, :] += mul(p, g)
            return dq_t + mul(kt[c], ds)

        dq_t = lax.fori_loop(0, NKC, step, jnp.zeros((HD, 256), F32), unroll=UN)
        dq = (dq_t.T * FACTOR).astype(BF16)
        one, two = block_of(b)
        xx[one[1], one[0], :, pl.ds(0, HD)] = dq[:SH]
        xx[two[1], two[0], :, pl.ds(0, HD)] = dq[SH:]

    loads[2].wait()
    wo_copy.wait_recv()

    def attn_grad(d):
        two = 0 < d < 4
        if two:
            tokens = jnp.concatenate([gath[zmod(z + d)], gath[zmod(z - d)]], axis=0)
        else:
            tokens = gath[zmod(z + d)]
        count = 2 * SH if two else SH
        res = mul_t(tokens, w2[...]).astype(BF16)
        gsend[d, pl.ds(0, count)] = res[:, HD:]
        g_copy(d, two).start()
        blk = 2 * d - 1 if d else 0
        gblk[blk, pl.ds(0, count)] = res[:, :HD]

    def arrived(pos):
        for way in (0, 1):
            ag_in(way, jnp.int32(pos)).wait_recv()

    attn_grad(0)
    attn_grad(1)

    @pl.loop(0, 8)
    def _(j):
        @pl.when(j == 1)
        def _():
            g_copy(0, False).wait_recv()

        @pl.when(j == 2)
        def _():
            forward(jnp.int32(2))
            g_copy(1, True).wait_recv()

        @pl.when(j == 3)
        def _():
            forward(jnp.int32(3))
            attn_grad(2)

        @pl.when(j == 4)
        def _():
            forward(jnp.int32(4))
            g_copy(2, True).wait_recv()

        @pl.when(j == 5)
        def _():
            arrived(5)
            attn_grad(3)

        @pl.when(j == 6)
        def _():
            arrived(6)
            attn_grad(4)
            g_copy(3, True).wait_recv()

        @pl.when(j == 7)
        def _():
            g_copy(4, False).wait_recv()

        wq_copy(4 + j).start()
        first = 1 - lax.div(j + 6, 8)
        backward_block(j + first * (1 - 2 * j))

    def x_copy(zz):
        return pltpu.make_async_remote_copy(
            src_ref=xx.at[1, zz],
            dst_ref=xpar.at[zz],
            send_sem=x_s.at[zz],
            recv_sem=x_r.at[zz],
            device_id=partner,
            device_id_type=MESH,
        )

    def place(zz, far):
        rows = token_rows(zz, far)
        xx[far, zz, :, pl.ds(HD, HD)] = (dk_acc[rows, :] * FACTOR).astype(BF16)
        xx[far, zz, :, pl.ds(2 * HD, HD)] = dv_acc[rows, :].astype(BF16)

    def in_order(i):
        away = 4 - lax.div(i + 1, 2)
        return zmod(z + away * (2 * lax.rem(i, 2) - 1))

    place(in_order(jnp.int32(0)), 1)
    x_copy(in_order(jnp.int32(0))).start()

    @pl.loop(1, NZ)
    def _(i):
        place(in_order(i), 1)

    def start_x(i):
        x_copy(in_order(jnp.int32(i))).start()

    start_x(1)
    start_x(2)

    @pl.loop(0, NZ)
    def _(i):
        place(in_order(i), 0)

    loads[3].wait()

    @pl.loop(0, 12)
    def _(i):
        wq_copy(i).wait_recv()

    def shard_x(zz):
        return jnp.concatenate([xx[0, zz], xpar[zz]], axis=1)

    def product(x, rows):
        @pl.loop(0, D // 512)
        def _(n):
            cols = pl.ds(pl.multiple_of(n * 512, 512), 512)
            w = wcat[:, :, cols].reshape(6 * HD, 512)
            ybuf[pl.ds(0, rows), cols] = mul(x, w)

    def rs_copy(way, pos):
        return pltpu.make_async_remote_copy(
            src_ref=rsend.at[way, pos],
            dst_ref=rrecv.at[way, pos],
            send_sem=rs_s.at[way, pos],
            recv_sem=rs_r.at[way, pos],
            device_id=z_to[way],
            device_id_type=MESH,
        )

    def piece(way, k):
        q = lax.rem(k, 2) if way else 1 - lax.rem(k, 2)
        return 2 * q + lax.div(k, 2)

    far4 = zmod(z + 4)
    x_copy(far4).wait_recv()
    start_x(3)
    start_x(4)
    product(shard_x(far4), SH)
    for k in (0, 1):
        for way in (0, 1):
            rsend[way, k] = ybuf[pl.ds((2 * way + k) * QR, QR), :].astype(BF16)
            rs_copy(way, k).start()

    loads[4].wait()
    loads[5].wait()

    @pl.loop(0, SH // QR)
    def _(i):
        rows = pl.ds(pl.multiple_of(i * QR, QR), QR)
        xv = bi_v[rows, :].astype(F32)
        centered = xv - jnp.mean(xv, axis=-1, keepdims=True)
        var = jnp.mean(centered * centered, axis=-1, keepdims=True)
        rstd = 1.0 / jnp.sqrt(var + EPS)
        xhat[rows, :] = centered * rstd
        rstd_v[rows, :] = jnp.broadcast_to(rstd, (QR, HD))

    def pair_product(d):
        plus, minus = zmod(z + d), zmod(z - d)
        x_copy(plus).wait_recv()
        x_copy(minus).wait_recv()

        @pl.when(d == 3)
        def _():
            start_x(5)
            start_x(6)

        @pl.when(d == 2)
        def _():
            start_x(7)

        product(jnp.concatenate([shard_x(plus), shard_x(minus)], axis=0), 2 * SH)

    def rows_of(way, k):
        return pl.ds(pl.multiple_of(way * SH + piece(way, k) * QR, QR), QR)

    def send_fresh(k):
        for way in (0, 1):
            rsend[way, 2 + k] = ybuf[rows_of(way, k), :].astype(BF16)
            rs_copy(way, 2 + k).start()

    def send_added(pos, k, came):
        for way in (0, 1):
            rs_copy(way, came).wait_recv()
            rsend[way, pos] = (ybuf[rows_of(way, k), :] + rrecv[way, came].astype(F32)).astype(BF16)
            rs_copy(way, pos).start()

    pair_product(jnp.int32(3))
    for k in range(4):
        if k % 2 == 0:
            send_fresh(k)
        else:
            send_added(2 + k, k, k // 2)

    @pl.loop(1, 3)
    def _(s):
        pair_product(3 - s)

        @pl.loop(0, 4)
        def _(k):
            pos = 2 + 4 * s + k
            send_added(pos, k, pos - 4)

    x_copy(z).wait_recv()
    product(shard_x(z), SH)

    one_scale = 1.0 + scale_ref[...]

    def next_copy(q):
        rows = pl.ds(pl.multiple_of(q * QR, QR), QR)
        return pltpu.make_async_remote_copy(
            src_ref=hand.at[rows],
            dst_ref=next_ref.at[rows],
            send_sem=nx_s.at[q],
            recv_sem=nx_r.at[q],
            device_id=(lax.rem(sec + 1, nsec), me),
            device_id_type=MESH,
        )

    def ig_copy(q):
        rows = pl.ds(pl.multiple_of(q * QR, QR), QR)
        return pltpu.make_async_copy(ig_v.at[rows], ig_ref.at[rows], ig_sem.at[q])

    def finish(q, plus_pos, minus_pos):
        rows = pl.ds(pl.multiple_of(q * QR, QR), QR)
        normed = ybuf[rows, :] + rrecv[0, plus_pos].astype(F32) + rrecv[1, minus_pos].astype(F32)
        xh = xhat[rows, :]
        scaled = normed * one_scale
        mean1 = jnp.mean(scaled, axis=-1, keepdims=True)
        mean2 = jnp.mean(scaled * xh, axis=-1, keepdims=True)
        rstd = rstd_v[rows, pl.ds(0, 1)]
        ig = go_v[rows, :].astype(F32) + rstd * (scaled - mean1 - xh * mean2)
        hand[rows, :] = ig.astype(BF16)
        if nsec > 1:

            @pl.when(sec < nsec - 1)
            def _():
                next_copy(q).start()

        ig_v[rows, :] = ig
        ig_copy(q).start()
        return jnp.sum(ig * sk_v[rows, :].astype(F32), axis=0, keepdims=True)

    gain_sum = jnp.zeros((1, D), F32)
    for j in (0, 1):
        for k in (2 * j, 2 * j + 1):
            for way in (0, 1):
                rs_copy(way, jnp.int32(10 + k)).wait_recv()
        gain_sum += finish(jnp.int32(j), 10 + 2 * j + 1, 10 + 2 * j)
        gain_sum += finish(jnp.int32(2 + j), 10 + 2 * j, 10 + 2 * j + 1)

    gslots[me] = gain_sum

    def gain_copy(off):
        return pltpu.make_async_remote_copy(
            src_ref=gslots.at[me],
            dst_ref=gslots.at[me],
            send_sem=gg_s.at[off],
            recv_sem=gg_r.at[off],
            device_id=(sec, lax.rem(me + off, 2 * NZ)),
            device_id_type=MESH,
        )

    def gain_in(off):
        came = lax.rem(me - off + 2 * NZ, 2 * NZ)
        return pltpu.make_async_remote_copy(
            src_ref=gslots.at[came],
            dst_ref=gslots.at[came],
            send_sem=gg_s.at[off],
            recv_sem=gg_r.at[off],
            device_id=(sec, lax.rem(me + off, 2 * NZ)),
            device_id_type=MESH,
        )

    @pl.loop(1, 2 * NZ)
    def _(off):
        gain_copy(off).start()

    @pl.loop(0, 7)
    def _(pos):
        for way in (0, 1):
            ag_out(way, pos).wait_send()

    @pl.loop(1, 2 * NZ)
    def _(off):
        gain_in(off).wait_recv()

    gg_ref[...] = jnp.sum(gslots[...], axis=0)

    wo_copy.wait_send()

    @pl.loop(0, 12)
    def _(i):
        wq_copy(i).wait_send()

    for d in range(5):
        g_copy(d, 0 < d < 4).wait_send()

    @pl.loop(0, NZ)
    def _(i):
        x_copy(i).wait_send()

    @pl.loop(0, 14)
    def _(pos):
        for way in (0, 1):
            rs_copy(way, pos).wait_send()

    @pl.loop(0, 4)
    def _(q):
        ig_copy(q).wait()

    @pl.loop(1, 2 * NZ)
    def _(off):
        gain_copy(off).wait_send()

    if nsec > 1:

        @pl.when(sec < nsec - 1)
        def _():
            @pl.loop(0, 4)
            def _(q):
                next_copy(q).wait_send()

        @pl.when(sec > 0)
        def _():
            @pl.loop(0, 4)
            def _(q):
                next_copy(q).wait_recv()


def on_device(nsec, go, bi, sk, qkv, wo, wq, gate, scale, gain):
    any_spec = pl.BlockSpec(memory_space=pl.ANY)
    vmem_spec = pl.BlockSpec(memory_space=pltpu.VMEM)
    dma = pltpu.SemaphoreType.DMA
    nxt, ig, gg = pl.pallas_call(
        functools.partial(kernel, nsec),
        out_shape=(
            jax.ShapeDtypeStruct((SH, D), BF16),
            jax.ShapeDtypeStruct((SH, D), F32),
            jax.ShapeDtypeStruct((1, D), F32),
        ),
        in_specs=[any_spec] * 6 + [vmem_spec] * 2,
        out_specs=(any_spec, any_spec, vmem_spec),
        scratch_shapes=[
            pltpu.VMEM((SH, D), BF16),
            pltpu.VMEM((SH, D), BF16),
            pltpu.VMEM((SH, D), BF16),
            pltpu.VMEM((3, T, HD), BF16),
            pltpu.VMEM((2 * SH, D), BF16),
            pltpu.VMEM((6, HD, D), BF16),
            pltpu.VMEM((NZ, SH, D), BF16),
            pltpu.VMEM((T, 256), F32),
            pltpu.VMEM((8, T, 256), BF16),
            pltpu.VMEM((8, 256, HD), F32),
            pltpu.VMEM((NKC, HD, KC), BF16),
            pltpu.VMEM((NKC, HD, KC), BF16),
            pltpu.VMEM((T, 2 * HD), BF16),
            pltpu.VMEM((8, 256, HD), BF16),
            pltpu.VMEM((5, 256, HD), BF16),
            pltpu.VMEM((T, HD), F32),
            pltpu.VMEM((T, HD), F32),
            pltpu.VMEM((2, NZ, SH, 3 * HD), BF16),
            pltpu.VMEM((NZ, SH, 3 * HD), BF16),
            pltpu.VMEM((2 * SH, D), F32),
            pltpu.VMEM((2, 14, QR, D), BF16),
            pltpu.VMEM((2, 14, QR, D), BF16),
            pltpu.VMEM((SH, D), F32),
            pltpu.VMEM((SH, HD), F32),
            pltpu.VMEM((SH, D), BF16),
            pltpu.VMEM((SH, D), F32),
            pltpu.VMEM((2 * NZ, 1, D), F32),
            dma((6,)),
            dma((2, 7)),
            dma((2, 7)),
            dma,
            dma,
            dma((12,)),
            dma((12,)),
            dma((5,)),
            dma((5,)),
            dma((NZ,)),
            dma((NZ,)),
            dma((2, 14)),
            dma((2, 14)),
            dma((4,)),
            dma((4,)),
            dma((4,)),
            dma((2 * NZ,)),
            dma((2 * NZ,)),
        ],
        compiler_params=pltpu.CompilerParams(
            collective_id=0, has_side_effects=True, vmem_limit_bytes=56 * 2**20
        ),
    )(go[0], bi[0], sk[0], qkv[0], wo[0], wq[0], gate, scale)
    sec = lax.axis_index("section")
    nxt = jnp.where(sec == 0, jnp.zeros_like(nxt), nxt)
    last = jnp.where(sec == nsec - 1, 1.0, 0.0).astype(F32)
    down = ((gain + last) * ig).astype(BF16)
    return nxt[None], down[None], gg


def solution(mesh):
    in_specs = (
        P("section", "seq", None),
        P("section", "seq", None),
        P("section", "seq", None),
        P("section", None, None, "seq"),
        P("section", "seq", None),
        P("section", None, "seq", None),
        P("section", None),
        P("section", None),
        P("section", None),
    )
    out_specs = (P("section", "seq", None), P("section", "seq", None), P("section", None))
    return jax.shard_map(
        functools.partial(on_device, mesh.shape["section"]),
        mesh=mesh,
        in_specs=in_specs,
        out_specs=out_specs,
        check_vma=False,
    )
```

```python
import functools

import jax
import jax.numpy as jnp
from jax import lax
from jax.experimental import pallas as pl
from jax.experimental.pallas import tpu as pltpu
from jax.sharding import PartitionSpec as P

F32 = jnp.float32
BF16 = jnp.bfloat16
MESH = pl.DeviceIdType.MESH

HD = 128
NZ = 8
SH = 128
D = 2048
T = 2048
KC = 256
NKC = T // KC
UN = 8
QR = 32
EPS = 1e-6
FACTOR = HD**-0.5


def mul_t(a, b):
    return lax.dot_general(a, b, (((1,), (1,)), ((), ())), preferred_element_type=F32)


def mul(a, b):
    return jnp.dot(a, b, preferred_element_type=F32)


def kernel(
    nsec,
    go_ref,
    bi_ref,
    sk_ref,
    qkv_ref,
    wo_ref,
    wq_ref,
    gate_ref,
    scale_ref,
    next_ref,
    ig_ref,
    gg_ref,
    go_v,
    bi_v,
    sk_v,
    qkv_v,
    w2,
    wcat,
    gath,
    sbuf,
    pbuf,
    obuf,
    kt,
    vt,
    vaug,
    gblk,
    gsend,
    dk_acc,
    dv_acc,
    xx,
    xpar,
    ybuf,
    rsend,
    rrecv,
    xhat,
    rstd_v,
    hand,
    ig_v,
    gslots,
    ld_sem,
    ag_s,
    ag_r,
    wo_s,
    wo_r,
    wq_s,
    wq_r,
    g_s,
    g_r,
    x_s,
    x_r,
    rs_s,
    rs_r,
    nx_s,
    nx_r,
    ig_sem,
    gg_s,
    gg_r,
):
    sec = lax.axis_index("section")
    me = lax.axis_index("seq")
    z = lax.div(me, 2)
    y = lax.rem(me, 2)

    def zmod(v):
        return lax.rem(v + 2 * NZ, NZ)

    def dev(zz, yy):
        return (sec, zz * 2 + yy)

    z_to = (dev(zmod(z + 1), y), dev(zmod(z - 1), y))
    partner = dev(z, 1 - y)

    loads = [
        pltpu.make_async_copy(src, dst, ld_sem.at[i])
        for i, (src, dst) in enumerate(
            [
                (go_ref, go_v),
                (qkv_ref, qkv_v),
                (wo_ref, w2.at[pl.ds(0, SH)]),
                (wq_ref, wcat.at[pl.ds(0, 3)]),
                (bi_ref, bi_v),
                (sk_ref, sk_v),
            ]
        )
    ]
    loads[0].start()

    barrier = pltpu.get_barrier_semaphore()

    @pl.loop(1, 2 * NZ)
    def _(off):
        pl.semaphore_signal(
            barrier, inc=1, device_id=(sec, lax.rem(me + off, 2 * NZ)), device_id_type=MESH
        )

    greeted = 2 * NZ - 1
    if nsec > 1:
        for step in (1, nsec - 1):
            pl.semaphore_signal(
                barrier, inc=1, device_id=(lax.rem(sec + step, nsec), me), device_id_type=MESH
            )
        greeted += 2

    loads[0].wait()
    for copy in loads[1:]:
        copy.start()
    gath[z] = (go_v[...].astype(F32) * gate_ref[...]).astype(BF16)
    pl.semaphore_wait(barrier, greeted)

    def ag_copy(way, pos, shard):
        half = lax.rem(pos, 2) if way == 0 else 1 - lax.rem(pos, 2)
        part = gath.at[shard, pl.ds(pl.multiple_of(half * (SH // 2), SH // 2), SH // 2)]
        return pltpu.make_async_remote_copy(
            src_ref=part,
            dst_ref=part,
            send_sem=ag_s.at[way, pos],
            recv_sem=ag_r.at[way, pos],
            device_id=z_to[way],
            device_id_type=MESH,
        )

    def ag_out(way, pos):
        back = lax.div(pos, 2)
        return ag_copy(way, pos, zmod(z - back) if way == 0 else zmod(z + back))

    def ag_in(way, pos):
        back = lax.div(pos, 2) + 1
        return ag_copy(way, pos, zmod(z - back) if way == 0 else zmod(z + back))

    for pos in (0, 1):
        for way in (0, 1):
            ag_out(way, jnp.int32(pos)).start()

    def forward(pos):
        for way in (0, 1):
            ag_in(way, pos).wait_recv()
            ag_out(way, pos + 2).start()

    wo_copy = pltpu.make_async_remote_copy(
        src_ref=wo_ref,
        dst_ref=w2.at[pl.ds(SH, SH)],
        send_sem=wo_s,
        recv_sem=wo_r,
        device_id=partner,
        device_id_type=MESH,
    )
    wo_copy.start()

    def wq_copy(i):
        which = lax.div(i, 4)
        rows = pl.ds(pl.multiple_of(lax.rem(i, 4) * 32, 32), 32)
        return pltpu.make_async_remote_copy(
            src_ref=wq_ref.at[which, rows],
            dst_ref=wcat.at[3 + which, rows],
            send_sem=wq_s.at[i],
            recv_sem=wq_r.at[i],
            device_id=partner,
            device_id_type=MESH,
        )

    loads[1].wait()
    lanes = lax.broadcasted_iota(jnp.int32, (KC, HD), 1)
    eye = (
        lax.broadcasted_iota(jnp.int32, (HD, HD), 0)
        == lax.broadcasted_iota(jnp.int32, (HD, HD), 1)
    ).astype(F32).astype(BF16)
    ones2 = (lanes < 2).astype(F32).astype(BF16)

    @pl.loop(0, NKC)
    def _(c):
        rows = pl.ds(pl.multiple_of(c * KC, KC), KC)
        kk = qkv_v[1, rows]
        vv = qkv_v[2, rows]
        kt[c] = mul_t(eye, kk).astype(BF16)
        vt[c] = mul_t(eye, vv).astype(BF16)
        vaug[rows, pl.ds(0, HD)] = vv
        vaug[rows, pl.ds(HD, HD)] = ones2

    def block_of(b):
        d = lax.div(b + 1, 2)
        odd = lax.rem(b, 2)
        far1 = (1 - odd) * lax.div(b + 6, 7)
        far2 = 1 - odd * (1 - lax.div(b, 7))
        return (zmod(z + d), far1), (zmod(z - d), far2)

    def token_rows(zz, far):
        shard = zz * 2 + lax.rem(y + far, 2)
        return pl.ds(pl.multiple_of(shard * SH, SH), SH)

    def queries(b):
        one, two = block_of(b)
        return jnp.concatenate([qkv_v[0, token_rows(*one)], qkv_v[0, token_rows(*two)]], axis=0)

    def softmax_block(b):
        qb = queries(b)

        def scores(c, top):
            rows = pl.ds(pl.multiple_of(c * KC, KC), KC)
            s = mul_t(qkv_v[1, rows], qb)
            sbuf[rows, :] = s
            return jnp.maximum(top, s.reshape(KC // 8, 8, 256).max(axis=0))

        top = lax.fori_loop(0, NKC, scores, jnp.full((8, 256), -jnp.inf, F32), unroll=UN)
        top = jnp.max(top, axis=0, keepdims=True)

        def weights(c, total):
            rows = pl.ds(pl.multiple_of(c * KC, KC), KC)
            e = jnp.exp((sbuf[rows, :] - top) * FACTOR)
            sbuf[rows, :] = e
            return total + e.reshape(KC // 8, 8, 256).sum(axis=0)

        total = lax.fori_loop(0, NKC, weights, jnp.zeros((8, 256), F32), unroll=UN)
        inverse = 1.0 / jnp.sum(total, axis=0, keepdims=True)

        def output(c, acc):
            rows = pl.ds(pl.multiple_of(c * KC, KC), KC)
            p = (sbuf[rows, :] * inverse).astype(BF16)
            pbuf[b, rows, :] = p
            return acc + mul(vt[c], p)

        out_t = lax.fori_loop(0, NKC, output, jnp.zeros((HD, 256), F32), unroll=UN)
        obuf[b] = out_t.T

    dk_acc[...] = jnp.zeros_like(dk_acc)
    dv_acc[...] = jnp.zeros_like(dv_acc)

    @pl.loop(0, 8)
    def _(b):
        softmax_block(b)

        @pl.when(lax.rem(b, 3) == 2)
        def _():
            forward(lax.div(b, 3))

        @pl.when(b > 2)
        def _():
            wq_copy(b - 3).start()

    def g_copy(d, two):
        if two:
            src, dst = gsend.at[d], gblk.at[2 * d]
        else:
            blk = 0 if d == 0 else 7
            src, dst = gsend.at[d, pl.ds(0, SH)], gblk.at[blk, pl.ds(SH, SH)]
        return pltpu.make_async_remote_copy(
            src_ref=src,
            dst_ref=dst,
            send_sem=g_s.at[d],
            recv_sem=g_r.at[d],
            device_id=partner,
            device_id_type=MESH,
        )

    def backward_block(b):
        qb = queries(b)
        g = gblk[b]
        delta = jnp.sum(g.astype(F32) * obuf[b], axis=1, keepdims=True)
        high = delta.astype(BF16).astype(F32)
        low = delta - high
        extra = jnp.where(lanes == 0, -high, jnp.where(lanes == 1, -low, 0.0)).astype(BF16)
        gaug = jnp.concatenate([g, extra], axis=1)

        def step(c, dq_t):
            rows = pl.ds(pl.multiple_of(c * KC, KC), KC)
            p = pbuf[b, rows, :]
            ds = (p.astype(F32) * mul_t(vaug[rows, :], gaug)).astype(BF16)
            dk_acc[rows, :] += mul(ds, qb)
            dv_acc[rows, :] += mul(p, g)
            return dq_t + mul(kt[c], ds)

        dq_t = lax.fori_loop(0, NKC, step, jnp.zeros((HD, 256), F32), unroll=UN)
        dq = (dq_t.T * FACTOR).astype(BF16)
        one, two = block_of(b)
        xx[one[1], one[0], :, pl.ds(0, HD)] = dq[:SH]
        xx[two[1], two[0], :, pl.ds(0, HD)] = dq[SH:]

    loads[2].wait()
    wo_copy.wait_recv()

    def attn_grad(d):
        two = 0 < d < 4
        if two:
            tokens = jnp.concatenate([gath[zmod(z + d)], gath[zmod(z - d)]], axis=0)
        else:
            tokens = gath[zmod(z + d)]
        count = 2 * SH if two else SH
        res = mul_t(tokens, w2[...]).astype(BF16)
        gsend[d, pl.ds(0, count)] = res[:, HD:]
        g_copy(d, two).start()
        blk = 2 * d - 1 if d else 0
        gblk[blk, pl.ds(0, count)] = res[:, :HD]

    def arrived(pos):
        for way in (0, 1):
            ag_in(way, jnp.int32(pos)).wait_recv()

    attn_grad(0)
    attn_grad(1)

    @pl.loop(0, 8)
    def _(j):
        @pl.when(j == 1)
        def _():
            g_copy(0, False).wait_recv()

        @pl.when(j == 2)
        def _():
            forward(jnp.int32(2))
            g_copy(1, True).wait_recv()

        @pl.when(j == 3)
        def _():
            forward(jnp.int32(3))
            attn_grad(2)

        @pl.when(j == 4)
        def _():
            forward(jnp.int32(4))
            g_copy(2, True).wait_recv()

        @pl.when(j == 5)
        def _():
            arrived(5)
            attn_grad(3)

        @pl.when(j == 6)
        def _():
            arrived(6)
            attn_grad(4)
            g_copy(3, True).wait_recv()

        @pl.when(j == 7)
        def _():
            g_copy(4, False).wait_recv()

        @pl.when(j < 6)
        def _():
            wq_copy(5 + j).start()

        @pl.when(j == 3)
        def _():
            wq_copy(jnp.int32(11)).start()

        first = 1 - lax.div(j + 6, 8)
        backward_block(j + first * (1 - 2 * j))

    def x_copy(zz):
        return pltpu.make_async_remote_copy(
            src_ref=xx.at[1, zz],
            dst_ref=xpar.at[zz],
            send_sem=x_s.at[zz],
            recv_sem=x_r.at[zz],
            device_id=partner,
            device_id_type=MESH,
        )

    def place(zz, far):
        rows = token_rows(zz, far)
        xx[far, zz, :, pl.ds(HD, HD)] = (dk_acc[rows, :] * FACTOR).astype(BF16)
        xx[far, zz, :, pl.ds(2 * HD, HD)] = dv_acc[rows, :].astype(BF16)

    def in_order(i):
        away = 4 - lax.div(i + 1, 2)
        return zmod(z + away * (2 * lax.rem(i, 2) - 1))

    place(in_order(jnp.int32(0)), 1)
    x_copy(in_order(jnp.int32(0))).start()

    @pl.loop(1, NZ)
    def _(i):
        place(in_order(i), 1)

    def start_x(i):
        x_copy(in_order(jnp.int32(i))).start()

    start_x(1)
    start_x(2)

    @pl.loop(0, NZ)
    def _(i):
        place(in_order(i), 0)

    loads[3].wait()

    @pl.loop(0, 12)
    def _(i):
        wq_copy(i).wait_recv()

    def shard_x(zz):
        return jnp.concatenate([xx[0, zz], xpar[zz]], axis=1)

    def product(x, rows):
        @pl.loop(0, D // 512)
        def _(n):
            cols = pl.ds(pl.multiple_of(n * 512, 512), 512)
            w = wcat[:, :, cols].reshape(6 * HD, 512)
            ybuf[pl.ds(0, rows), cols] = mul(x, w)

    def rs_copy(way, pos):
        return pltpu.make_async_remote_copy(
            src_ref=rsend.at[way, pos],
            dst_ref=rrecv.at[way, pos],
            send_sem=rs_s.at[way, pos],
            recv_sem=rs_r.at[way, pos],
            device_id=z_to[way],
            device_id_type=MESH,
        )

    def piece(way, k):
        q = lax.rem(k, 2) if way else 1 - lax.rem(k, 2)
        return 2 * q + lax.div(k, 2)

    far4 = zmod(z + 4)
    x_copy(far4).wait_recv()
    start_x(3)
    start_x(4)
    product(shard_x(far4), SH)
    for k in (0, 1):
        for way in (0, 1):
            rsend[way, k] = ybuf[pl.ds((2 * way + k) * QR, QR), :].astype(BF16)
            rs_copy(way, k).start()

    loads[4].wait()
    loads[5].wait()

    @pl.loop(0, SH // QR)
    def _(i):
        rows = pl.ds(pl.multiple_of(i * QR, QR), QR)
        xv = bi_v[rows, :].astype(F32)
        centered = xv - jnp.mean(xv, axis=-1, keepdims=True)
        var = jnp.mean(centered * centered, axis=-1, keepdims=True)
        rstd = 1.0 / jnp.sqrt(var + EPS)
        xhat[rows, :] = centered * rstd
        rstd_v[rows, :] = jnp.broadcast_to(rstd, (QR, HD))

    def pair_product(d):
        plus, minus = zmod(z + d), zmod(z - d)
        x_copy(plus).wait_recv()
        x_copy(minus).wait_recv()

        @pl.when(d == 3)
        def _():
            start_x(5)
            start_x(6)

        @pl.when(d == 2)
        def _():
            start_x(7)

        product(jnp.concatenate([shard_x(plus), shard_x(minus)], axis=0), 2 * SH)

    def rows_of(way, k):
        return pl.ds(pl.multiple_of(way * SH + piece(way, k) * QR, QR), QR)

    def send_fresh(k):
        for way in (0, 1):
            rsend[way, 2 + k] = ybuf[rows_of(way, k), :].astype(BF16)
            rs_copy(way, 2 + k).start()

    def send_added(pos, k, came):
        for way in (0, 1):
            rs_copy(way, came).wait_recv()
            rsend[way, pos] = (ybuf[rows_of(way, k), :] + rrecv[way, came].astype(F32)).astype(BF16)
            rs_copy(way, pos).start()

    pair_product(jnp.int32(3))
    for k in range(4):
        if k % 2 == 0:
            send_fresh(k)
        else:
            send_added(2 + k, k, k // 2)

    @pl.loop(1, 3)
    def _(s):
        pair_product(3 - s)

        @pl.loop(0, 4)
        def _(k):
            pos = 2 + 4 * s + k
            send_added(pos, k, pos - 4)

    x_copy(z).wait_recv()
    product(shard_x(z), SH)

    one_scale = 1.0 + scale_ref[...]

    def next_copy(q):
        rows = pl.ds(pl.multiple_of(q * QR, QR), QR)
        return pltpu.make_async_remote_copy(
            src_ref=hand.at[rows],
            dst_ref=next_ref.at[rows],
            send_sem=nx_s.at[q],
            recv_sem=nx_r.at[q],
            device_id=(lax.rem(sec + 1, nsec), me),
            device_id_type=MESH,
        )

    def ig_copy(q):
        rows = pl.ds(pl.multiple_of(q * QR, QR), QR)
        return pltpu.make_async_copy(ig_v.at[rows], ig_ref.at[rows], ig_sem.at[q])

    def finish(q, plus_pos, minus_pos):
        rows = pl.ds(pl.multiple_of(q * QR, QR), QR)
        normed = ybuf[rows, :] + rrecv[0, plus_pos].astype(F32) + rrecv[1, minus_pos].astype(F32)
        xh = xhat[rows, :]
        scaled = normed * one_scale
        mean1 = jnp.mean(scaled, axis=-1, keepdims=True)
        mean2 = jnp.mean(scaled * xh, axis=-1, keepdims=True)
        rstd = rstd_v[rows, pl.ds(0, 1)]
        ig = go_v[rows, :].astype(F32) + rstd * (scaled - mean1 - xh * mean2)
        hand[rows, :] = ig.astype(BF16)
        if nsec > 1:

            @pl.when(sec < nsec - 1)
            def _():
                next_copy(q).start()

        ig_v[rows, :] = ig
        ig_copy(q).start()
        return jnp.sum(ig * sk_v[rows, :].astype(F32), axis=0, keepdims=True)

    gain_sum = jnp.zeros((1, D), F32)
    for j in (0, 1):
        for k in (2 * j, 2 * j + 1):
            for way in (0, 1):
                rs_copy(way, jnp.int32(10 + k)).wait_recv()
        gain_sum += finish(jnp.int32(j), 10 + 2 * j + 1, 10 + 2 * j)
        gain_sum += finish(jnp.int32(2 + j), 10 + 2 * j, 10 + 2 * j + 1)

    gslots[me] = gain_sum

    def gain_copy(off):
        return pltpu.make_async_remote_copy(
            src_ref=gslots.at[me],
            dst_ref=gslots.at[me],
            send_sem=gg_s.at[off],
            recv_sem=gg_r.at[off],
            device_id=(sec, lax.rem(me + off, 2 * NZ)),
            device_id_type=MESH,
        )

    def gain_in(off):
        came = lax.rem(me - off + 2 * NZ, 2 * NZ)
        return pltpu.make_async_remote_copy(
            src_ref=gslots.at[came],
            dst_ref=gslots.at[came],
            send_sem=gg_s.at[off],
            recv_sem=gg_r.at[off],
            device_id=(sec, lax.rem(me + off, 2 * NZ)),
            device_id_type=MESH,
        )

    @pl.loop(1, 2 * NZ)
    def _(off):
        gain_copy(off).start()

    @pl.loop(0, 7)
    def _(pos):
        for way in (0, 1):
            ag_out(way, pos).wait_send()

    @pl.loop(1, 2 * NZ)
    def _(off):
        gain_in(off).wait_recv()

    gg_ref[...] = jnp.sum(gslots[...], axis=0)

    wo_copy.wait_send()

    @pl.loop(0, 12)
    def _(i):
        wq_copy(i).wait_send()

    for d in range(5):
        g_copy(d, 0 < d < 4).wait_send()

    @pl.loop(0, NZ)
    def _(i):
        x_copy(i).wait_send()

    @pl.loop(0, 14)
    def _(pos):
        for way in (0, 1):
            rs_copy(way, pos).wait_send()

    @pl.loop(0, 4)
    def _(q):
        ig_copy(q).wait()

    @pl.loop(1, 2 * NZ)
    def _(off):
        gain_copy(off).wait_send()

    if nsec > 1:

        @pl.when(sec < nsec - 1)
        def _():
            @pl.loop(0, 4)
            def _(q):
                next_copy(q).wait_send()

        @pl.when(sec > 0)
        def _():
            @pl.loop(0, 4)
            def _(q):
                next_copy(q).wait_recv()


def on_device(nsec, go, bi, sk, qkv, wo, wq, gate, scale, gain):
    any_spec = pl.BlockSpec(memory_space=pl.ANY)
    vmem_spec = pl.BlockSpec(memory_space=pltpu.VMEM)
    dma = pltpu.SemaphoreType.DMA
    nxt, ig, gg = pl.pallas_call(
        functools.partial(kernel, nsec),
        out_shape=(
            jax.ShapeDtypeStruct((SH, D), BF16),
            jax.ShapeDtypeStruct((SH, D), F32),
            jax.ShapeDtypeStruct((1, D), F32),
        ),
        in_specs=[any_spec] * 6 + [vmem_spec] * 2,
        out_specs=(any_spec, any_spec, vmem_spec),
        scratch_shapes=[
            pltpu.VMEM((SH, D), BF16),
            pltpu.VMEM((SH, D), BF16),
            pltpu.VMEM((SH, D), BF16),
            pltpu.VMEM((3, T, HD), BF16),
            pltpu.VMEM((2 * SH, D), BF16),
            pltpu.VMEM((6, HD, D), BF16),
            pltpu.VMEM((NZ, SH, D), BF16),
            pltpu.VMEM((T, 256), F32),
            pltpu.VMEM((8, T, 256), BF16),
            pltpu.VMEM((8, 256, HD), F32),
            pltpu.VMEM((NKC, HD, KC), BF16),
            pltpu.VMEM((NKC, HD, KC), BF16),
            pltpu.VMEM((T, 2 * HD), BF16),
            pltpu.VMEM((8, 256, HD), BF16),
            pltpu.VMEM((5, 256, HD), BF16),
            pltpu.VMEM((T, HD), F32),
            pltpu.VMEM((T, HD), F32),
            pltpu.VMEM((2, NZ, SH, 3 * HD), BF16),
            pltpu.VMEM((NZ, SH, 3 * HD), BF16),
            pltpu.VMEM((2 * SH, D), F32),
            pltpu.VMEM((2, 14, QR, D), BF16),
            pltpu.VMEM((2, 14, QR, D), BF16),
            pltpu.VMEM((SH, D), F32),
            pltpu.VMEM((SH, HD), F32),
            pltpu.VMEM((SH, D), BF16),
            pltpu.VMEM((SH, D), F32),
            pltpu.VMEM((2 * NZ, 1, D), F32),
            dma((6,)),
            dma((2, 7)),
            dma((2, 7)),
            dma,
            dma,
            dma((12,)),
            dma((12,)),
            dma((5,)),
            dma((5,)),
            dma((NZ,)),
            dma((NZ,)),
            dma((2, 14)),
            dma((2, 14)),
            dma((4,)),
            dma((4,)),
            dma((4,)),
            dma((2 * NZ,)),
            dma((2 * NZ,)),
        ],
        compiler_params=pltpu.CompilerParams(
            collective_id=0, has_side_effects=True, vmem_limit_bytes=56 * 2**20
        ),
    )(go[0], bi[0], sk[0], qkv[0], wo[0], wq[0], gate, scale)
    sec = lax.axis_index("section")
    nxt = jnp.where(sec == 0, jnp.zeros_like(nxt), nxt)
    last = jnp.where(sec == nsec - 1, 1.0, 0.0).astype(F32)
    down = ((gain + last) * ig).astype(BF16)
    return nxt[None], down[None], gg


def solution(mesh):
    in_specs = (
        P("section", "seq", None),
        P("section", "seq", None),
        P("section", "seq", None),
        P("section", None, None, "seq"),
        P("section", "seq", None),
        P("section", None, "seq", None),
        P("section", None),
        P("section", None),
        P("section", None),
    )
    out_specs = (P("section", "seq", None), P("section", "seq", None), P("section", None))
    return jax.shard_map(
        functools.partial(on_device, mesh.shape["section"]),
        mesh=mesh,
        in_specs=in_specs,
        out_specs=out_specs,
        check_vma=False,
    )
```

```python
import functools

import jax
import jax.numpy as jnp
from jax import lax
from jax.experimental import pallas as pl
from jax.experimental.pallas import tpu as pltpu
from jax.sharding import PartitionSpec as P

F32 = jnp.float32
BF16 = jnp.bfloat16
MESH = pl.DeviceIdType.MESH

HD = 128
NZ = 8
SH = 128
D = 2048
T = 2048
KC = 256
NKC = T // KC
UN = 8
QR = 32
EPS = 1e-6
FACTOR = HD**-0.5


def mul_t(a, b):
    return lax.dot_general(a, b, (((1,), (1,)), ((), ())), preferred_element_type=F32)


def mul(a, b):
    return jnp.dot(a, b, preferred_element_type=F32)


def kernel(
    nsec,
    go_ref,
    bi_ref,
    sk_ref,
    qkv_ref,
    wo_ref,
    wq_ref,
    gate_ref,
    scale_ref,
    next_ref,
    ig_ref,
    gg_ref,
    go_v,
    bi_v,
    sk_v,
    qkv_v,
    w2,
    wcat,
    gath,
    sbuf,
    pbuf,
    obuf,
    kt,
    vt,
    vaug,
    gblk,
    gsend,
    dk_acc,
    dv_acc,
    xx,
    xpar,
    ybuf,
    rsend,
    rrecv,
    xhat,
    rstd_v,
    hand,
    ig_v,
    gslots,
    ld_sem,
    ag_s,
    ag_r,
    wo_s,
    wo_r,
    wq_s,
    wq_r,
    g_s,
    g_r,
    x_s,
    x_r,
    rs_s,
    rs_r,
    nx_s,
    nx_r,
    ig_sem,
    gg_s,
    gg_r,
):
    sec = lax.axis_index("section")
    me = lax.axis_index("seq")
    z = lax.div(me, 2)
    y = lax.rem(me, 2)

    def zmod(v):
        return lax.rem(v + 2 * NZ, NZ)

    def dev(zz, yy):
        return (sec, zz * 2 + yy)

    z_to = (dev(zmod(z + 1), y), dev(zmod(z - 1), y))
    partner = dev(z, 1 - y)

    loads = [
        pltpu.make_async_copy(src, dst, ld_sem.at[i])
        for i, (src, dst) in enumerate(
            [
                (go_ref, go_v),
                (qkv_ref, qkv_v),
                (wo_ref, w2.at[pl.ds(0, SH)]),
                (wq_ref, wcat.at[pl.ds(0, 3)]),
                (bi_ref, bi_v),
                (sk_ref, sk_v),
            ]
        )
    ]
    for copy in loads:
        copy.start()

    barrier = pltpu.get_barrier_semaphore()

    @pl.loop(1, 2 * NZ)
    def _(off):
        pl.semaphore_signal(
            barrier, inc=1, device_id=(sec, lax.rem(me + off, 2 * NZ)), device_id_type=MESH
        )

    greeted = 2 * NZ - 1
    if nsec > 1:
        for step in (1, nsec - 1):
            pl.semaphore_signal(
                barrier, inc=1, device_id=(lax.rem(sec + step, nsec), me), device_id_type=MESH
            )
        greeted += 2

    loads[0].wait()
    gath[z] = (go_v[...].astype(F32) * gate_ref[...]).astype(BF16)
    pl.semaphore_wait(barrier, greeted)

    def ag_copy(way, pos, shard):
        half = lax.rem(pos, 2) if way == 0 else 1 - lax.rem(pos, 2)
        part = gath.at[shard, pl.ds(pl.multiple_of(half * (SH // 2), SH // 2), SH // 2)]
        return pltpu.make_async_remote_copy(
            src_ref=part,
            dst_ref=part,
            send_sem=ag_s.at[way, pos],
            recv_sem=ag_r.at[way, pos],
            device_id=z_to[way],
            device_id_type=MESH,
        )

    def ag_out(way, pos):
        back = lax.div(pos, 2)
        return ag_copy(way, pos, zmod(z - back) if way == 0 else zmod(z + back))

    def ag_in(way, pos):
        back = lax.div(pos, 2) + 1
        return ag_copy(way, pos, zmod(z - back) if way == 0 else zmod(z + back))

    for pos in (0, 1):
        for way in (0, 1):
            ag_out(way, jnp.int32(pos)).start()

    def forward(pos):
        for way in (0, 1):
            ag_in(way, pos).wait_recv()
            ag_out(way, pos + 2).start()

    wo_copy = pltpu.make_async_remote_copy(
        src_ref=wo_ref,
        dst_ref=w2.at[pl.ds(SH, SH)],
        send_sem=wo_s,
        recv_sem=wo_r,
        device_id=partner,
        device_id_type=MESH,
    )
    wo_copy.start()

    def wq_copy(i):
        which = lax.div(i, 4)
        rows = pl.ds(pl.multiple_of(lax.rem(i, 4) * 32, 32), 32)
        return pltpu.make_async_remote_copy(
            src_ref=wq_ref.at[which, rows],
            dst_ref=wcat.at[3 + which, rows],
            send_sem=wq_s.at[i],
            recv_sem=wq_r.at[i],
            device_id=partner,
            device_id_type=MESH,
        )

    loads[1].wait()
    lanes = lax.broadcasted_iota(jnp.int32, (KC, HD), 1)
    eye = (
        lax.broadcasted_iota(jnp.int32, (HD, HD), 0)
        == lax.broadcasted_iota(jnp.int32, (HD, HD), 1)
    ).astype(F32).astype(BF16)
    ones2 = (lanes < 2).astype(F32).astype(BF16)

    @pl.loop(0, NKC)
    def _(c):
        rows = pl.ds(pl.multiple_of(c * KC, KC), KC)
        kk = qkv_v[1, rows]
        vv = qkv_v[2, rows]
        kt[c] = mul_t(eye, kk).astype(BF16)
        vt[c] = mul_t(eye, vv).astype(BF16)
        vaug[rows, pl.ds(0, HD)] = vv
        vaug[rows, pl.ds(HD, HD)] = ones2

    def block_of(b):
        d = lax.div(b + 1, 2)
        odd = lax.rem(b, 2)
        far1 = (1 - odd) * lax.div(b + 6, 7)
        far2 = 1 - odd * (1 - lax.div(b, 7))
        return (zmod(z + d), far1), (zmod(z - d), far2)

    def token_rows(zz, far):
        shard = zz * 2 + lax.rem(y + far, 2)
        return pl.ds(pl.multiple_of(shard * SH, SH), SH)

    def queries(b):
        one, two = block_of(b)
        return jnp.concatenate([qkv_v[0, token_rows(*one)], qkv_v[0, token_rows(*two)]], axis=0)

    def softmax_block(b):
        qb = queries(b)

        def scores(c, top):
            rows = pl.ds(pl.multiple_of(c * KC, KC), KC)
            s = mul_t(qkv_v[1, rows], qb)
            sbuf[rows, :] = s
            return jnp.maximum(top, s.reshape(KC // 8, 8, 256).max(axis=0))

        top = lax.fori_loop(0, NKC, scores, jnp.full((8, 256), -jnp.inf, F32), unroll=UN)
        top = jnp.max(top, axis=0, keepdims=True)

        def weights(c, total):
            rows = pl.ds(pl.multiple_of(c * KC, KC), KC)
            e = jnp.exp((sbuf[rows, :] - top) * FACTOR)
            sbuf[rows, :] = e
            return total + e.reshape(KC // 8, 8, 256).sum(axis=0)

        total = lax.fori_loop(0, NKC, weights, jnp.zeros((8, 256), F32), unroll=UN)
        inverse = 1.0 / jnp.sum(total, axis=0, keepdims=True)

        def output(c, acc):
            rows = pl.ds(pl.multiple_of(c * KC, KC), KC)
            p = (sbuf[rows, :] * inverse).astype(BF16)
            pbuf[b, rows, :] = p
            return acc + mul(vt[c], p)

        out_t = lax.fori_loop(0, NKC, output, jnp.zeros((HD, 256), F32), unroll=UN)
        obuf[b] = out_t.T

    dk_acc[...] = jnp.zeros_like(dk_acc)
    dv_acc[...] = jnp.zeros_like(dv_acc)

    @pl.loop(0, 8)
    def _(b):
        softmax_block(b)

        @pl.when(jnp.logical_and(lax.rem(b, 3) == 0, b > 0))
        def _():
            forward(lax.div(b, 3) - 1)

        @pl.when(b > 3)
        def _():
            wq_copy(b - 4).start()

    def g_copy(d, two):
        if two:
            src, dst = gsend.at[d], gblk.at[2 * d]
        else:
            blk = 0 if d == 0 else 7
            src, dst = gsend.at[d, pl.ds(0, SH)], gblk.at[blk, pl.ds(SH, SH)]
        return pltpu.make_async_remote_copy(
            src_ref=src,
            dst_ref=dst,
            send_sem=g_s.at[d],
            recv_sem=g_r.at[d],
            device_id=partner,
            device_id_type=MESH,
        )

    def backward_block(b):
        qb = queries(b)
        g = gblk[b]
        delta = jnp.sum(g.astype(F32) * obuf[b], axis=1, keepdims=True)
        high = delta.astype(BF16).astype(F32)
        low = delta - high
        extra = jnp.where(lanes == 0, -high, jnp.where(lanes == 1, -low, 0.0)).astype(BF16)
        gaug = jnp.concatenate([g, extra], axis=1)

        def step(c, dq_t):
            rows = pl.ds(pl.multiple_of(c * KC, KC), KC)
            p = pbuf[b, rows, :]
            ds = (p.astype(F32) * mul_t(vaug[rows, :], gaug)).astype(BF16)
            dk_acc[rows, :] += mul(ds, qb)
            dv_acc[rows, :] += mul(p, g)
            return dq_t + mul(kt[c], ds)

        dq_t = lax.fori_loop(0, NKC, step, jnp.zeros((HD, 256), F32), unroll=UN)
        dq = (dq_t.T * FACTOR).astype(BF16)
        one, two = block_of(b)
        xx[one[1], one[0], :, pl.ds(0, HD)] = dq[:SH]
        xx[two[1], two[0], :, pl.ds(0, HD)] = dq[SH:]

    loads[2].wait()
    wo_copy.wait_recv()

    def attn_grad(d):
        two = 0 < d < 4
        if two:
            tokens = jnp.concatenate([gath[zmod(z + d)], gath[zmod(z - d)]], axis=0)
        else:
            tokens = gath[zmod(z + d)]
        count = 2 * SH if two else SH
        res = mul_t(tokens, w2[...]).astype(BF16)
        gsend[d, pl.ds(0, count)] = res[:, HD:]
        g_copy(d, two).start()
        blk = 2 * d - 1 if d else 0
        gblk[blk, pl.ds(0, count)] = res[:, :HD]

    def arrived(pos):
        for way in (0, 1):
            ag_in(way, jnp.int32(pos)).wait_recv()

    attn_grad(0)
    attn_grad(1)

    @pl.loop(0, 8)
    def _(j):
        @pl.when(j == 1)
        def _():
            g_copy(0, False).wait_recv()

        @pl.when(j == 2)
        def _():
            forward(jnp.int32(2))
            g_copy(1, True).wait_recv()

        @pl.when(j == 3)
        def _():
            forward(jnp.int32(3))
            attn_grad(2)

        @pl.when(j == 4)
        def _():
            forward(jnp.int32(4))
            g_copy(2, True).wait_recv()

        @pl.when(j == 5)
        def _():
            arrived(5)
            attn_grad(3)

        @pl.when(j == 6)
        def _():
            arrived(6)
            attn_grad(4)
            g_copy(3, True).wait_recv()

        @pl.when(j == 7)
        def _():
            g_copy(4, False).wait_recv()

        wq_copy(4 + j).start()
        first = 1 - lax.div(j + 6, 8)
        backward_block(j + first * (1 - 2 * j))

    def x_copy(zz):
        return pltpu.make_async_remote_copy(
            src_ref=xx.at[1, zz],
            dst_ref=xpar.at[zz],
            send_sem=x_s.at[zz],
            recv_sem=x_r.at[zz],
            device_id=partner,
            device_id_type=MESH,
        )

    def place(zz, far):
        rows = token_rows(zz, far)
        xx[far, zz, :, pl.ds(HD, HD)] = (dk_acc[rows, :] * FACTOR).astype(BF16)
        xx[far, zz, :, pl.ds(2 * HD, HD)] = dv_acc[rows, :].astype(BF16)

    def in_order(i):
        away = 4 - lax.div(i + 1, 2)
        return zmod(z + away * (2 * lax.rem(i, 2) - 1))

    place(in_order(jnp.int32(0)), 1)
    x_copy(in_order(jnp.int32(0))).start()

    @pl.loop(1, NZ)
    def _(i):
        place(in_order(i), 1)

    def start_x(i):
        x_copy(in_order(jnp.int32(i))).start()

    start_x(1)
    start_x(2)

    @pl.loop(0, NZ)
    def _(i):
        place(in_order(i), 0)

    loads[3].wait()

    @pl.loop(0, 12)
    def _(i):
        wq_copy(i).wait_recv()

    def shard_x(zz):
        return jnp.concatenate([xx[0, zz], xpar[zz]], axis=1)

    def product(x, rows):
        @pl.loop(0, D // 512)
        def _(n):
            cols = pl.ds(pl.multiple_of(n * 512, 512), 512)
            w = wcat[:, :, cols].reshape(6 * HD, 512)
            ybuf[pl.ds(0, rows), cols] = mul(x, w)

    def rs_copy(way, pos):
        return pltpu.make_async_remote_copy(
            src_ref=rsend.at[way, pos],
            dst_ref=rrecv.at[way, pos],
            send_sem=rs_s.at[way, pos],
            recv_sem=rs_r.at[way, pos],
            device_id=z_to[way],
            device_id_type=MESH,
        )

    def piece(way, k):
        q = lax.rem(k, 2) if way else 1 - lax.rem(k, 2)
        return 2 * q + lax.div(k, 2)

    far4 = zmod(z + 4)
    x_copy(far4).wait_recv()
    start_x(3)
    start_x(4)
    product(shard_x(far4), SH)
    for k in (0, 1):
        for way in (0, 1):
            rsend[way, k] = ybuf[pl.ds((2 * way + k) * QR, QR), :].astype(BF16)
            rs_copy(way, k).start()

    loads[4].wait()
    loads[5].wait()

    @pl.loop(0, SH // QR)
    def _(i):
        rows = pl.ds(pl.multiple_of(i * QR, QR), QR)
        xv = bi_v[rows, :].astype(F32)
        centered = xv - jnp.mean(xv, axis=-1, keepdims=True)
        var = jnp.mean(centered * centered, axis=-1, keepdims=True)
        rstd = 1.0 / jnp.sqrt(var + EPS)
        xhat[rows, :] = centered * rstd
        rstd_v[rows, :] = jnp.broadcast_to(rstd, (QR, HD))

    def pair_product(d):
        plus, minus = zmod(z + d), zmod(z - d)
        x_copy(plus).wait_recv()
        x_copy(minus).wait_recv()

        @pl.when(d == 3)
        def _():
            start_x(5)
            start_x(6)

        @pl.when(d == 2)
        def _():
            start_x(7)

        product(jnp.concatenate([shard_x(plus), shard_x(minus)], axis=0), 2 * SH)

    def rows_of(way, k):
        return pl.ds(pl.multiple_of(way * SH + piece(way, k) * QR, QR), QR)

    def send_fresh(k):
        for way in (0, 1):
            rsend[way, 2 + k] = ybuf[rows_of(way, k), :].astype(BF16)
            rs_copy(way, 2 + k).start()

    def send_added(pos, k, came):
        for way in (0, 1):
            rs_copy(way, came).wait_recv()
            rsend[way, pos] = (ybuf[rows_of(way, k), :] + rrecv[way, came].astype(F32)).astype(BF16)
            rs_copy(way, pos).start()

    pair_product(jnp.int32(3))
    for k in range(4):
        if k % 2 == 0:
            send_fresh(k)
        else:
            send_added(2 + k, k, k // 2)

    @pl.loop(1, 3)
    def _(s):
        pair_product(3 - s)

        @pl.loop(0, 4)
        def _(k):
            pos = 2 + 4 * s + k
            send_added(pos, k, pos - 4)

    x_copy(z).wait_recv()
    product(shard_x(z), SH)

    one_scale = 1.0 + scale_ref[...]

    def next_copy(q):
        rows = pl.ds(pl.multiple_of(q * QR, QR), QR)
        return pltpu.make_async_remote_copy(
            src_ref=hand.at[rows],
            dst_ref=next_ref.at[rows],
            send_sem=nx_s.at[q],
            recv_sem=nx_r.at[q],
            device_id=(lax.rem(sec + 1, nsec), me),
            device_id_type=MESH,
        )

    def ig_copy(q):
        rows = pl.ds(pl.multiple_of(q * QR, QR), QR)
        return pltpu.make_async_copy(ig_v.at[rows], ig_ref.at[rows], ig_sem.at[q])

    def finish(q, plus_pos, minus_pos):
        rows = pl.ds(pl.multiple_of(q * QR, QR), QR)
        normed = ybuf[rows, :] + rrecv[0, plus_pos].astype(F32) + rrecv[1, minus_pos].astype(F32)
        xh = xhat[rows, :]
        scaled = normed * one_scale
        mean1 = jnp.mean(scaled, axis=-1, keepdims=True)
        mean2 = jnp.mean(scaled * xh, axis=-1, keepdims=True)
        rstd = rstd_v[rows, pl.ds(0, 1)]
        ig = go_v[rows, :].astype(F32) + rstd * (scaled - mean1 - xh * mean2)
        hand[rows, :] = ig.astype(BF16)
        if nsec > 1:

            @pl.when(sec < nsec - 1)
            def _():
                next_copy(q).start()

        ig_v[rows, :] = ig
        ig_copy(q).start()
        return jnp.sum(ig * sk_v[rows, :].astype(F32), axis=0, keepdims=True)

    gain_sum = jnp.zeros((1, D), F32)
    for j in (0, 1):
        for k in (2 * j, 2 * j + 1):
            for way in (0, 1):
                rs_copy(way, jnp.int32(10 + k)).wait_recv()
        gain_sum += finish(jnp.int32(j), 10 + 2 * j + 1, 10 + 2 * j)
        gain_sum += finish(jnp.int32(2 + j), 10 + 2 * j, 10 + 2 * j + 1)

    gslots[me] = gain_sum

    def gain_copy(off):
        return pltpu.make_async_remote_copy(
            src_ref=gslots.at[me],
            dst_ref=gslots.at[me],
            send_sem=gg_s.at[off],
            recv_sem=gg_r.at[off],
            device_id=(sec, lax.rem(me + off, 2 * NZ)),
            device_id_type=MESH,
        )

    def gain_in(off):
        came = lax.rem(me - off + 2 * NZ, 2 * NZ)
        return pltpu.make_async_remote_copy(
            src_ref=gslots.at[came],
            dst_ref=gslots.at[came],
            send_sem=gg_s.at[off],
            recv_sem=gg_r.at[off],
            device_id=(sec, lax.rem(me + off, 2 * NZ)),
            device_id_type=MESH,
        )

    @pl.loop(1, 2 * NZ)
    def _(off):
        gain_copy(off).start()

    @pl.loop(0, 7)
    def _(pos):
        for way in (0, 1):
            ag_out(way, pos).wait_send()

    @pl.loop(1, 2 * NZ)
    def _(off):
        gain_in(off).wait_recv()

    gg_ref[...] = jnp.sum(gslots[...], axis=0)

    wo_copy.wait_send()

    @pl.loop(0, 12)
    def _(i):
        wq_copy(i).wait_send()

    for d in range(5):
        g_copy(d, 0 < d < 4).wait_send()

    @pl.loop(0, NZ)
    def _(i):
        x_copy(i).wait_send()

    @pl.loop(0, 14)
    def _(pos):
        for way in (0, 1):
            rs_copy(way, pos).wait_send()

    @pl.loop(0, 4)
    def _(q):
        ig_copy(q).wait()

    @pl.loop(1, 2 * NZ)
    def _(off):
        gain_copy(off).wait_send()

    if nsec > 1:

        @pl.when(sec < nsec - 1)
        def _():
            @pl.loop(0, 4)
            def _(q):
                next_copy(q).wait_send()

        @pl.when(sec > 0)
        def _():
            @pl.loop(0, 4)
            def _(q):
                next_copy(q).wait_recv()


def on_device(nsec, go, bi, sk, qkv, wo, wq, gate, scale, gain):
    any_spec = pl.BlockSpec(memory_space=pl.ANY)
    vmem_spec = pl.BlockSpec(memory_space=pltpu.VMEM)
    dma = pltpu.SemaphoreType.DMA
    nxt, ig, gg = pl.pallas_call(
        functools.partial(kernel, nsec),
        out_shape=(
            jax.ShapeDtypeStruct((SH, D), BF16),
            jax.ShapeDtypeStruct((SH, D), F32),
            jax.ShapeDtypeStruct((1, D), F32),
        ),
        in_specs=[any_spec] * 6 + [vmem_spec] * 2,
        out_specs=(any_spec, any_spec, vmem_spec),
        scratch_shapes=[
            pltpu.VMEM((SH, D), BF16),
            pltpu.VMEM((SH, D), BF16),
            pltpu.VMEM((SH, D), BF16),
            pltpu.VMEM((3, T, HD), BF16),
            pltpu.VMEM((2 * SH, D), BF16),
            pltpu.VMEM((6, HD, D), BF16),
            pltpu.VMEM((NZ, SH, D), BF16),
            pltpu.VMEM((T, 256), F32),
            pltpu.VMEM((8, T, 256), BF16),
            pltpu.VMEM((8, 256, HD), F32),
            pltpu.VMEM((NKC, HD, KC), BF16),
            pltpu.VMEM((NKC, HD, KC), BF16),
            pltpu.VMEM((T, 2 * HD), BF16),
            pltpu.VMEM((8, 256, HD), BF16),
            pltpu.VMEM((5, 256, HD), BF16),
            pltpu.VMEM((T, HD), F32),
            pltpu.VMEM((T, HD), F32),
            pltpu.VMEM((2, NZ, SH, 3 * HD), BF16),
            pltpu.VMEM((NZ, SH, 3 * HD), BF16),
            pltpu.VMEM((2 * SH, D), F32),
            pltpu.VMEM((2, 14, QR, D), BF16),
            pltpu.VMEM((2, 14, QR, D), BF16),
            pltpu.VMEM((SH, D), F32),
            pltpu.VMEM((SH, HD), F32),
            pltpu.VMEM((SH, D), BF16),
            pltpu.VMEM((SH, D), F32),
            pltpu.VMEM((2 * NZ, 1, D), F32),
            dma((6,)),
            dma((2, 7)),
            dma((2, 7)),
            dma,
            dma,
            dma((12,)),
            dma((12,)),
            dma((5,)),
            dma((5,)),
            dma((NZ,)),
            dma((NZ,)),
            dma((2, 14)),
            dma((2, 14)),
            dma((4,)),
            dma((4,)),
            dma((4,)),
            dma((2 * NZ,)),
            dma((2 * NZ,)),
        ],
        compiler_params=pltpu.CompilerParams(
            collective_id=0, has_side_effects=True, vmem_limit_bytes=56 * 2**20
        ),
    )(go[0], bi[0], sk[0], qkv[0], wo[0], wq[0], gate, scale)
    sec = lax.axis_index("section")
    nxt = jnp.where(sec == 0, jnp.zeros_like(nxt), nxt)
    last = jnp.where(sec == nsec - 1, 1.0, 0.0).astype(F32)
    down = ((gain + last) * ig).astype(BF16)
    return nxt[None], down[None], gg


def solution(mesh):
    in_specs = (
        P("section", "seq", None),
        P("section", "seq", None),
        P("section", "seq", None),
        P("section", None, None, "seq"),
        P("section", "seq", None),
        P("section", None, "seq", None),
        P("section", None),
        P("section", None),
        P("section", None),
    )
    out_specs = (P("section", "seq", None), P("section", "seq", None), P("section", None))
    return jax.shard_map(
        functools.partial(on_device, mesh.shape["section"]),
        mesh=mesh,
        in_specs=in_specs,
        out_specs=out_specs,
        check_vma=False,
    )
```

```python
import functools

import jax
import jax.numpy as jnp
from jax import lax
from jax.experimental import pallas as pl
from jax.experimental.pallas import tpu as pltpu
from jax.sharding import PartitionSpec as P

F32 = jnp.float32
BF16 = jnp.bfloat16
MESH = pl.DeviceIdType.MESH

HD = 128
NZ = 8
SH = 128
D = 2048
T = 2048
KC = 256
NKC = T // KC
UN = 8
QR = 32
EPS = 1e-6
FACTOR = HD**-0.5


def mul_t(a, b):
    return lax.dot_general(a, b, (((1,), (1,)), ((), ())), preferred_element_type=F32)


def mul(a, b):
    return jnp.dot(a, b, preferred_element_type=F32)


def kernel(
    nsec,
    go_ref,
    bi_ref,
    sk_ref,
    qkv_ref,
    wo_ref,
    wq_ref,
    gate_ref,
    scale_ref,
    next_ref,
    ig_ref,
    gg_ref,
    go_v,
    bi_v,
    sk_v,
    qkv_v,
    w2,
    wcat,
    gath,
    sbuf,
    pbuf,
    obuf,
    kt,
    vt,
    vaug,
    gblk,
    gsend,
    dk_acc,
    dv_acc,
    xx,
    xpar,
    ybuf,
    rsend,
    rrecv,
    xhat,
    rstd_v,
    hand,
    ig_v,
    gslots,
    ld_sem,
    ag_s,
    ag_r,
    wo_s,
    wo_r,
    wq_s,
    wq_r,
    g_s,
    g_r,
    x_s,
    x_r,
    rs_s,
    rs_r,
    nx_s,
    nx_r,
    ig_sem,
    gg_s,
    gg_r,
):
    sec = lax.axis_index("section")
    me = lax.axis_index("seq")
    z = lax.div(me, 2)
    y = lax.rem(me, 2)

    def zmod(v):
        return lax.rem(v + 2 * NZ, NZ)

    def dev(zz, yy):
        return (sec, zz * 2 + yy)

    z_to = (dev(zmod(z + 1), y), dev(zmod(z - 1), y))
    partner = dev(z, 1 - y)

    loads = [
        pltpu.make_async_copy(src, dst, ld_sem.at[i])
        for i, (src, dst) in enumerate(
            [
                (go_ref, go_v),
                (qkv_ref, qkv_v),
                (wo_ref, w2.at[pl.ds(0, SH)]),
                (wq_ref, wcat.at[pl.ds(0, 3)]),
                (bi_ref, bi_v),
                (sk_ref, sk_v),
            ]
        )
    ]
    for copy in loads:
        copy.start()

    barrier = pltpu.get_barrier_semaphore()

    @pl.loop(1, 2 * NZ)
    def _(off):
        pl.semaphore_signal(
            barrier, inc=1, device_id=(sec, lax.rem(me + off, 2 * NZ)), device_id_type=MESH
        )

    greeted = 2 * NZ - 1
    if nsec > 1:
        for step in (1, nsec - 1):
            pl.semaphore_signal(
                barrier, inc=1, device_id=(lax.rem(sec + step, nsec), me), device_id_type=MESH
            )
        greeted += 2

    loads[0].wait()
    gath[z] = (go_v[...].astype(F32) * gate_ref[...]).astype(BF16)
    pl.semaphore_wait(barrier, greeted)

    def ag_copy(way, pos, shard):
        half = lax.rem(pos, 2) if way == 0 else 1 - lax.rem(pos, 2)
        part = gath.at[shard, pl.ds(pl.multiple_of(half * (SH // 2), SH // 2), SH // 2)]
        return pltpu.make_async_remote_copy(
            src_ref=part,
            dst_ref=part,
            send_sem=ag_s.at[way, pos],
            recv_sem=ag_r.at[way, pos],
            device_id=z_to[way],
            device_id_type=MESH,
        )

    def ag_out(way, pos):
        back = lax.div(pos, 2)
        return ag_copy(way, pos, zmod(z - back) if way == 0 else zmod(z + back))

    def ag_in(way, pos):
        back = lax.div(pos, 2) + 1
        return ag_copy(way, pos, zmod(z - back) if way == 0 else zmod(z + back))

    for pos in (0, 1):
        for way in (0, 1):
            ag_out(way, jnp.int32(pos)).start()

    def forward(pos):
        for way in (0, 1):
            ag_in(way, pos).wait_recv()
            ag_out(way, pos + 2).start()

    wo_copy = pltpu.make_async_remote_copy(
        src_ref=wo_ref,
        dst_ref=w2.at[pl.ds(SH, SH)],
        send_sem=wo_s,
        recv_sem=wo_r,
        device_id=partner,
        device_id_type=MESH,
    )
    wo_copy.start()

    def wq_copy(i):
        which = lax.div(i, 4)
        rows = pl.ds(pl.multiple_of(lax.rem(i, 4) * 32, 32), 32)
        return pltpu.make_async_remote_copy(
            src_ref=wq_ref.at[which, rows],
            dst_ref=wcat.at[3 + which, rows],
            send_sem=wq_s.at[i],
            recv_sem=wq_r.at[i],
            device_id=partner,
            device_id_type=MESH,
        )

    loads[1].wait()
    lanes = lax.broadcasted_iota(jnp.int32, (KC, HD), 1)
    eye = (
        lax.broadcasted_iota(jnp.int32, (HD, HD), 0)
        == lax.broadcasted_iota(jnp.int32, (HD, HD), 1)
    ).astype(F32).astype(BF16)
    ones2 = (lanes < 2).astype(F32).astype(BF16)

    @pl.loop(0, NKC)
    def _(c):
        rows = pl.ds(pl.multiple_of(c * KC, KC), KC)
        kk = qkv_v[1, rows]
        vv = qkv_v[2, rows]
        kt[c] = mul_t(eye, kk).astype(BF16)
        vt[c] = mul_t(eye, vv).astype(BF16)
        vaug[rows, pl.ds(0, HD)] = vv
        vaug[rows, pl.ds(HD, HD)] = ones2

    def block_of(b):
        d = lax.div(b + 1, 2)
        odd = lax.rem(b, 2)
        far1 = (1 - odd) * lax.div(b + 6, 7)
        far2 = 1 - odd * (1 - lax.div(b, 7))
        return (zmod(z + d), far1), (zmod(z - d), far2)

    def token_rows(zz, far):
        shard = zz * 2 + lax.rem(y + far, 2)
        return pl.ds(pl.multiple_of(shard * SH, SH), SH)

    def queries(b):
        one, two = block_of(b)
        return jnp.concatenate([qkv_v[0, token_rows(*one)], qkv_v[0, token_rows(*two)]], axis=0)

    def softmax_block(b):
        qb = queries(b)

        def scores(c, top):
            rows = pl.ds(pl.multiple_of(c * KC, KC), KC)
            s = mul_t(qkv_v[1, rows], qb)
            sbuf[rows, :] = s
            return jnp.maximum(top, s.reshape(KC // 8, 8, 256).max(axis=0))

        top = lax.fori_loop(0, NKC, scores, jnp.full((8, 256), -jnp.inf, F32), unroll=UN)
        top = jnp.max(top, axis=0, keepdims=True)

        def weights(c, total):
            rows = pl.ds(pl.multiple_of(c * KC, KC), KC)
            e = jnp.exp((sbuf[rows, :] - top) * FACTOR)
            sbuf[rows, :] = e
            return total + e.reshape(KC // 8, 8, 256).sum(axis=0)

        total = lax.fori_loop(0, NKC, weights, jnp.zeros((8, 256), F32), unroll=UN)
        inverse = 1.0 / jnp.sum(total, axis=0, keepdims=True)

        def output(c, acc):
            rows = pl.ds(pl.multiple_of(c * KC, KC), KC)
            p = (sbuf[rows, :] * inverse).astype(BF16)
            pbuf[b, rows, :] = p
            return acc + mul(vt[c], p)

        out_t = lax.fori_loop(0, NKC, output, jnp.zeros((HD, 256), F32), unroll=UN)
        obuf[b] = out_t.T

    dk_acc[...] = jnp.zeros_like(dk_acc)
    dv_acc[...] = jnp.zeros_like(dv_acc)

    @pl.loop(0, 8)
    def _(b):
        softmax_block(b)

        @pl.when(jnp.logical_and(lax.rem(b, 3) == 0, b > 0))
        def _():
            forward(lax.div(b, 3) - 1)

        @pl.when(b > 3)
        def _():
            wq_copy(b - 4).start()

    def g_copy(d, two):
        if two:
            src, dst = gsend.at[d], gblk.at[2 * d]
        else:
            blk = 0 if d == 0 else 7
            src, dst = gsend.at[d, pl.ds(0, SH)], gblk.at[blk, pl.ds(SH, SH)]
        return pltpu.make_async_remote_copy(
            src_ref=src,
            dst_ref=dst,
            send_sem=g_s.at[d],
            recv_sem=g_r.at[d],
            device_id=partner,
            device_id_type=MESH,
        )

    def backward_block(b):
        qb = queries(b)
        g = gblk[b]
        delta = jnp.sum(g.astype(F32) * obuf[b], axis=1, keepdims=True)
        high = delta.astype(BF16).astype(F32)
        low = delta - high
        extra = jnp.where(lanes == 0, -high, jnp.where(lanes == 1, -low, 0.0)).astype(BF16)
        gaug = jnp.concatenate([g, extra], axis=1)

        def step(c, dq_t):
            rows = pl.ds(pl.multiple_of(c * KC, KC), KC)
            p = pbuf[b, rows, :]
            ds = (p.astype(F32) * mul_t(vaug[rows, :], gaug)).astype(BF16)
            dk_acc[rows, :] += mul(ds, qb)
            dv_acc[rows, :] += mul(p, g)
            return dq_t + mul(kt[c], ds)

        dq_t = lax.fori_loop(0, NKC, step, jnp.zeros((HD, 256), F32), unroll=UN)
        dq = (dq_t.T * FACTOR).astype(BF16)
        one, two = block_of(b)
        xx[one[1], one[0], :, pl.ds(0, HD)] = dq[:SH]
        xx[two[1], two[0], :, pl.ds(0, HD)] = dq[SH:]

    loads[2].wait()
    wo_copy.wait_recv()

    def attn_grad(d):
        two = 0 < d < 4
        if two:
            tokens = jnp.concatenate([gath[zmod(z + d)], gath[zmod(z - d)]], axis=0)
        else:
            tokens = gath[zmod(z + d)]
        count = 2 * SH if two else SH
        res = mul_t(tokens, w2[...]).astype(BF16)
        gsend[d, pl.ds(0, count)] = res[:, HD:]
        g_copy(d, two).start()
        blk = 2 * d - 1 if d else 0
        gblk[blk, pl.ds(0, count)] = res[:, :HD]

    def arrived(pos):
        for way in (0, 1):
            ag_in(way, jnp.int32(pos)).wait_recv()

    def layer_norm():
        loads[4].wait()
        loads[5].wait()

        @pl.loop(0, SH // QR)
        def _(i):
            rows = pl.ds(pl.multiple_of(i * QR, QR), QR)
            xv = bi_v[rows, :].astype(F32)
            centered = xv - jnp.mean(xv, axis=-1, keepdims=True)
            var = jnp.mean(centered * centered, axis=-1, keepdims=True)
            rstd = 1.0 / jnp.sqrt(var + EPS)
            xhat[rows, :] = centered * rstd
            rstd_v[rows, :] = jnp.broadcast_to(rstd, (QR, HD))

    attn_grad(0)
    attn_grad(1)

    @pl.loop(0, 8)
    def _(j):
        @pl.when(j == 1)
        def _():
            g_copy(0, False).wait_recv()

        @pl.when(j == 2)
        def _():
            forward(jnp.int32(2))
            g_copy(1, True).wait_recv()

        @pl.when(j == 3)
        def _():
            forward(jnp.int32(3))
            attn_grad(2)

        @pl.when(j == 4)
        def _():
            forward(jnp.int32(4))
            g_copy(2, True).wait_recv()

        @pl.when(j == 5)
        def _():
            layer_norm()
            arrived(5)
            attn_grad(3)

        @pl.when(j == 6)
        def _():
            arrived(6)
            attn_grad(4)
            g_copy(3, True).wait_recv()

        @pl.when(j == 7)
        def _():
            g_copy(4, False).wait_recv()

        wq_copy(4 + j).start()
        first = 1 - lax.div(j + 6, 8)
        backward_block(j + first * (1 - 2 * j))

    def x_copy(zz):
        return pltpu.make_async_remote_copy(
            src_ref=xx.at[1, zz],
            dst_ref=xpar.at[zz],
            send_sem=x_s.at[zz],
            recv_sem=x_r.at[zz],
            device_id=partner,
            device_id_type=MESH,
        )

    def place(zz, far):
        rows = token_rows(zz, far)
        xx[far, zz, :, pl.ds(HD, HD)] = (dk_acc[rows, :] * FACTOR).astype(BF16)
        xx[far, zz, :, pl.ds(2 * HD, HD)] = dv_acc[rows, :].astype(BF16)

    def in_order(i):
        away = 4 - lax.div(i + 1, 2)
        return zmod(z + away * (2 * lax.rem(i, 2) - 1))

    place(in_order(jnp.int32(0)), 1)
    x_copy(in_order(jnp.int32(0))).start()

    @pl.loop(1, NZ)
    def _(i):
        place(in_order(i), 1)

    def start_x(i):
        x_copy(in_order(jnp.int32(i))).start()

    start_x(1)
    start_x(2)

    @pl.loop(0, NZ)
    def _(i):
        place(in_order(i), 0)

    loads[3].wait()

    @pl.loop(0, 12)
    def _(i):
        wq_copy(i).wait_recv()

    def shard_x(zz):
        return jnp.concatenate([xx[0, zz], xpar[zz]], axis=1)

    def product(x, rows):
        @pl.loop(0, D // 512)
        def _(n):
            cols = pl.ds(pl.multiple_of(n * 512, 512), 512)
            w = wcat[:, :, cols].reshape(6 * HD, 512)
            ybuf[pl.ds(0, rows), cols] = mul(x, w)

    def rs_copy(way, pos):
        return pltpu.make_async_remote_copy(
            src_ref=rsend.at[way, pos],
            dst_ref=rrecv.at[way, pos],
            send_sem=rs_s.at[way, pos],
            recv_sem=rs_r.at[way, pos],
            device_id=z_to[way],
            device_id_type=MESH,
        )

    def piece(way, k):
        q = lax.rem(k, 2) if way else 1 - lax.rem(k, 2)
        return 2 * q + lax.div(k, 2)

    far4 = zmod(z + 4)
    x_copy(far4).wait_recv()
    start_x(3)
    start_x(4)
    product(shard_x(far4), SH)
    for k in (0, 1):
        for way in (0, 1):
            rsend[way, k] = ybuf[pl.ds((2 * way + k) * QR, QR), :].astype(BF16)
            rs_copy(way, k).start()

    def pair_product(d):
        plus, minus = zmod(z + d), zmod(z - d)
        x_copy(plus).wait_recv()
        x_copy(minus).wait_recv()

        @pl.when(d == 3)
        def _():
            start_x(5)
            start_x(6)

        @pl.when(d == 2)
        def _():
            start_x(7)

        product(jnp.concatenate([shard_x(plus), shard_x(minus)], axis=0), 2 * SH)

    def rows_of(way, k):
        return pl.ds(pl.multiple_of(way * SH + piece(way, k) * QR, QR), QR)

    def send_fresh(k):
        for way in (0, 1):
            rsend[way, 2 + k] = ybuf[rows_of(way, k), :].astype(BF16)
            rs_copy(way, 2 + k).start()

    def send_added(pos, k, came):
        for way in (0, 1):
            rs_copy(way, came).wait_recv()
            rsend[way, pos] = (ybuf[rows_of(way, k), :] + rrecv[way, came].astype(F32)).astype(BF16)
            rs_copy(way, pos).start()

    pair_product(jnp.int32(3))
    for k in range(4):
        if k % 2 == 0:
            send_fresh(k)
        else:
            send_added(2 + k, k, k // 2)

    @pl.loop(1, 3)
    def _(s):
        pair_product(3 - s)

        @pl.loop(0, 4)
        def _(k):
            pos = 2 + 4 * s + k
            send_added(pos, k, pos - 4)

    x_copy(z).wait_recv()
    product(shard_x(z), SH)

    one_scale = 1.0 + scale_ref[...]

    def next_copy(q):
        rows = pl.ds(pl.multiple_of(q * QR, QR), QR)
        return pltpu.make_async_remote_copy(
            src_ref=hand.at[rows],
            dst_ref=next_ref.at[rows],
            send_sem=nx_s.at[q],
            recv_sem=nx_r.at[q],
            device_id=(lax.rem(sec + 1, nsec), me),
            device_id_type=MESH,
        )

    def ig_copy(q):
        rows = pl.ds(pl.multiple_of(q * QR, QR), QR)
        return pltpu.make_async_copy(ig_v.at[rows], ig_ref.at[rows], ig_sem.at[q])

    def finish(q, plus_pos, minus_pos):
        rows = pl.ds(pl.multiple_of(q * QR, QR), QR)
        normed = ybuf[rows, :] + rrecv[0, plus_pos].astype(F32) + rrecv[1, minus_pos].astype(F32)
        xh = xhat[rows, :]
        scaled = normed * one_scale
        mean1 = jnp.mean(scaled, axis=-1, keepdims=True)
        mean2 = jnp.mean(scaled * xh, axis=-1, keepdims=True)
        rstd = rstd_v[rows, pl.ds(0, 1)]
        ig = go_v[rows, :].astype(F32) + rstd * (scaled - mean1 - xh * mean2)
        hand[rows, :] = ig.astype(BF16)
        if nsec > 1:

            @pl.when(sec < nsec - 1)
            def _():
                next_copy(q).start()

        ig_v[rows, :] = ig
        ig_copy(q).start()
        return jnp.sum(ig * sk_v[rows, :].astype(F32), axis=0, keepdims=True)

    gain_sum = jnp.zeros((1, D), F32)
    for j in (0, 1):
        for k in (2 * j, 2 * j + 1):
            for way in (0, 1):
                rs_copy(way, jnp.int32(10 + k)).wait_recv()
        gain_sum += finish(jnp.int32(j), 10 + 2 * j + 1, 10 + 2 * j)
        gain_sum += finish(jnp.int32(2 + j), 10 + 2 * j, 10 + 2 * j + 1)

    gslots[me] = gain_sum

    def gain_copy(off):
        return pltpu.make_async_remote_copy(
            src_ref=gslots.at[me],
            dst_ref=gslots.at[me],
            send_sem=gg_s.at[off],
            recv_sem=gg_r.at[off],
            device_id=(sec, lax.rem(me + off, 2 * NZ)),
            device_id_type=MESH,
        )

    def gain_in(off):
        came = lax.rem(me - off + 2 * NZ, 2 * NZ)
        return pltpu.make_async_remote_copy(
            src_ref=gslots.at[came],
            dst_ref=gslots.at[came],
            send_sem=gg_s.at[off],
            recv_sem=gg_r.at[off],
            device_id=(sec, lax.rem(me + off, 2 * NZ)),
            device_id_type=MESH,
        )

    @pl.loop(1, 2 * NZ)
    def _(off):
        gain_copy(off).start()

    @pl.loop(0, 7)
    def _(pos):
        for way in (0, 1):
            ag_out(way, pos).wait_send()

    @pl.loop(1, 2 * NZ)
    def _(off):
        gain_in(off).wait_recv()

    gg_ref[...] = jnp.sum(gslots[...], axis=0)

    wo_copy.wait_send()

    @pl.loop(0, 12)
    def _(i):
        wq_copy(i).wait_send()

    for d in range(5):
        g_copy(d, 0 < d < 4).wait_send()

    @pl.loop(0, NZ)
    def _(i):
        x_copy(i).wait_send()

    @pl.loop(0, 14)
    def _(pos):
        for way in (0, 1):
            rs_copy(way, pos).wait_send()

    @pl.loop(0, 4)
    def _(q):
        ig_copy(q).wait()

    @pl.loop(1, 2 * NZ)
    def _(off):
        gain_copy(off).wait_send()

    if nsec > 1:

        @pl.when(sec < nsec - 1)
        def _():
            @pl.loop(0, 4)
            def _(q):
                next_copy(q).wait_send()

        @pl.when(sec > 0)
        def _():
            @pl.loop(0, 4)
            def _(q):
                next_copy(q).wait_recv()


def on_device(nsec, go, bi, sk, qkv, wo, wq, gate, scale, gain):
    any_spec = pl.BlockSpec(memory_space=pl.ANY)
    vmem_spec = pl.BlockSpec(memory_space=pltpu.VMEM)
    dma = pltpu.SemaphoreType.DMA
    nxt, ig, gg = pl.pallas_call(
        functools.partial(kernel, nsec),
        out_shape=(
            jax.ShapeDtypeStruct((SH, D), BF16),
            jax.ShapeDtypeStruct((SH, D), F32),
            jax.ShapeDtypeStruct((1, D), F32),
        ),
        in_specs=[any_spec] * 6 + [vmem_spec] * 2,
        out_specs=(any_spec, any_spec, vmem_spec),
        scratch_shapes=[
            pltpu.VMEM((SH, D), BF16),
            pltpu.VMEM((SH, D), BF16),
            pltpu.VMEM((SH, D), BF16),
            pltpu.VMEM((3, T, HD), BF16),
            pltpu.VMEM((2 * SH, D), BF16),
            pltpu.VMEM((6, HD, D), BF16),
            pltpu.VMEM((NZ, SH, D), BF16),
            pltpu.VMEM((T, 256), F32),
            pltpu.VMEM((8, T, 256), BF16),
            pltpu.VMEM((8, 256, HD), F32),
            pltpu.VMEM((NKC, HD, KC), BF16),
            pltpu.VMEM((NKC, HD, KC), BF16),
            pltpu.VMEM((T, 2 * HD), BF16),
            pltpu.VMEM((8, 256, HD), BF16),
            pltpu.VMEM((5, 256, HD), BF16),
            pltpu.VMEM((T, HD), F32),
            pltpu.VMEM((T, HD), F32),
            pltpu.VMEM((2, NZ, SH, 3 * HD), BF16),
            pltpu.VMEM((NZ, SH, 3 * HD), BF16),
            pltpu.VMEM((2 * SH, D), F32),
            pltpu.VMEM((2, 14, QR, D), BF16),
            pltpu.VMEM((2, 14, QR, D), BF16),
            pltpu.VMEM((SH, D), F32),
            pltpu.VMEM((SH, HD), F32),
            pltpu.VMEM((SH, D), BF16),
            pltpu.VMEM((SH, D), F32),
            pltpu.VMEM((2 * NZ, 1, D), F32),
            dma((6,)),
            dma((2, 7)),
            dma((2, 7)),
            dma,
            dma,
            dma((12,)),
            dma((12,)),
            dma((5,)),
            dma((5,)),
            dma((NZ,)),
            dma((NZ,)),
            dma((2, 14)),
            dma((2, 14)),
            dma((4,)),
            dma((4,)),
            dma((4,)),
            dma((2 * NZ,)),
            dma((2 * NZ,)),
        ],
        compiler_params=pltpu.CompilerParams(
            collective_id=0, has_side_effects=True, vmem_limit_bytes=56 * 2**20
        ),
    )(go[0], bi[0], sk[0], qkv[0], wo[0], wq[0], gate, scale)
    sec = lax.axis_index("section")
    nxt = jnp.where(sec == 0, jnp.zeros_like(nxt), nxt)
    last = jnp.where(sec == nsec - 1, 1.0, 0.0).astype(F32)
    down = ((gain + last) * ig).astype(BF16)
    return nxt[None], down[None], gg


def solution(mesh):
    in_specs = (
        P("section", "seq", None),
        P("section", "seq", None),
        P("section", "seq", None),
        P("section", None, None, "seq"),
        P("section", "seq", None),
        P("section", None, "seq", None),
        P("section", None),
        P("section", None),
        P("section", None),
    )
    out_specs = (P("section", "seq", None), P("section", "seq", None), P("section", None))
    return jax.shard_map(
        functools.partial(on_device, mesh.shape["section"]),
        mesh=mesh,
        in_specs=in_specs,
        out_specs=out_specs,
        check_vma=False,
    )
```
